32 devices in a mesh: row: 8 (over y, x, core), col: 4 (over z).
Axes of the slice: x: 2, y: 2, z: 4, core: 2. Of those that a mesh axis runs over, the one named last changes fastest.
Arguments:
- fields: float32 [4, 16, 64, 512], P(None, 'row', None, 'col'), may hold values from -6 to 6
- diffusivity: float32 [4], replicated, may hold values from 0.05 to 0.3
- records: float32 [6, 262144], P(None, ('row', 'col')), may hold values from -6 to 6
- response_time: float32 [262144], P(('row', 'col')), may hold values from 0.5 to 4
- cell_index: int32 [262144], P(('row', 'col')), may hold values from 0 to 16383
- counts: int32 [32], P(('row', 'col')), may hold values from 4096 to 8192, as said below
- destination: int32 [262144], P(('row', 'col')), may hold values from 0 to 4, as said below
- slot: int32 [262144], P(('row', 'col')), may hold values from 0 to 255, as said below
Outputs:
- tendency: float32 [4, 16, 64, 512], P(None, 'row', None, 'col')
- kept: float32 [6, 262144], P(None, ('row', 'col'))
- arrivals: float32 [4, 6, 8192], P(None, None, ('row', 'col'))
The draws below stay inside these ranges and needn't reach their ends.
Inputs may be any that keep to these rules, and one draw needn't show every extreme that they name: `counts`: both wall rows of pencils are full. `destination`: only live particles leave; none leaves row index 0 downward or row index 7 upward. For each pencil and direction the leaving particles' slots are distinct; pencil 0 sends exactly 256 particles toward col index + 1; slot is 0 for particles that stay.
All inputs are finite; a program needn't handle non-finite values.
Results may differ from the reference program's by a relative error of at most 0.00009.
Values sent between devices are 32-bit elements; how exact they have to be, the bound alone decides.
No kernel may reach another device: no remote copies, remote signals or barrier semaphores. Data moves between devices by JAX's collectives and lax.ppermute only.
A program may use at most 192 MiB of HBM per device.

```python
import math
import jax
import jax.numpy as jnp
from jax import lax

YR = 2
ZC = 128
NX = 64
NY = 16
NZ = 512
PART_DEV = 8192
MIG = 256
PENCIL_ROWS = 8
PENCIL_COLS = 4
PARTICLES = 262144


def pencil_lists(key):
    pencils = PENCIL_ROWS * PENCIL_COLS
    keys = jax.random.split(jax.random.fold_in(key, 7), 3)
    rows_of = jnp.arange(pencils, dtype=jnp.int32) // PENCIL_COLS
    middle_row = (PENCIL_ROWS - 1) // 2
    gap_scale = max(middle_row, 1)
    wall_gap = jnp.minimum(jnp.minimum(rows_of, PENCIL_ROWS - 1 - rows_of), gap_scale)
    reduction = jax.random.randint(keys[0], (pencils,), 0, PART_DEV // 2 + 1, dtype=jnp.int32)
    reduction = reduction.at[middle_row * PENCIL_COLS].set(PART_DEV // 2)
    live_count = (PART_DEV - reduction * wall_gap // gap_scale).astype(jnp.int32)
    leave = jax.random.randint(keys[1], (pencils, 4), MIG // 3, MIG + 1, dtype=jnp.int32)
    leave = leave.at[:, 0].set(jnp.where(rows_of == PENCIL_ROWS - 1, 0, leave[:, 0]))
    leave = leave.at[:, 1].set(jnp.where(rows_of == 0, 0, leave[:, 1]))
    leave = leave.at[0, 2].set(MIG)
    orders = jax.vmap(lambda one_key: jax.random.permutation(one_key, PART_DEV))(jax.random.split(keys[2], pencils))
    orders = orders.astype(jnp.int32)
    local = jnp.arange(PART_DEV, dtype=jnp.int32)
    scores = jnp.where(local[None, :] < live_count[:, None], orders, orders + PART_DEV)
    ranking = jnp.argsort(jnp.argsort(scores, axis=1), axis=1).astype(jnp.int32)
    bounds = jnp.cumsum(leave, axis=1).astype(jnp.int32)
    group = jnp.sum((ranking[:, :, None] >= bounds[:, None, :]).astype(jnp.int32), axis=2).astype(jnp.int32)
    starts = bounds - leave
    first_slot = jnp.take_along_axis(starts, jnp.minimum(group, 3), axis=1)
    target = jnp.where(group < 4, group + 1, 0).astype(jnp.int32)
    place = jnp.where(group < 4, ranking - first_slot, 0).astype(jnp.int32)
    return (live_count, target.reshape(-1), place.reshape(-1))


def draw_counts(key, part):
    return pencil_lists(key)[0]


def draw_destination(key, part):
    return pencil_lists(key)[1]


def draw_slot(key, part):
    return pencil_lists(key)[2]


def place_ends(result, key, least, largest):
    spot = [jax.random.randint(jax.random.fold_in(key, axis), (), 0, length) for axis, length in enumerate(result.shape)]
    main_axis = result.shape.index(max(result.shape))
    beside = spot[:main_axis] + [(spot[main_axis] + 1) % result.shape[main_axis]] + spot[main_axis + 1:]
    return result.at[tuple(spot)].set(least).at[tuple(beside)].set(largest)


def block_scale(key, shape, pieces, least, high):
    loudness, own = 1.0, jax.random.fold_in(key, 6)
    for dim, shards_of in pieces:
        draws = jnp.exp(jax.random.uniform(jax.random.fold_in(own, dim), (shards_of,), jnp.float32, least / len(pieces), high / len(pieces)))
        loudness = loudness * jnp.repeat(draws, shape[dim] // shards_of).reshape([-1 if axis == dim else 1 for axis in range(len(shape))])
    return loudness


def bell_draw(key, shape, width, reach, shards=(), held_as=jnp.bfloat16):
    values = width * jax.random.normal(key, shape, jnp.float32)
    if shards:
        values = values * block_scale(key, shape, shards, -0.22, 0.18)
    return jnp.clip(values, -reach, reach).astype(held_as)


def setup_inputs(seed: int = 0) -> dict:
    key_of = jax.random.split(jax.random.key(seed), 9)
    return {
        "fields": bell_draw(key_of[0], (4, NY, NX, NZ), 1.0, 6.0, ((1, 8), (3, 4)), jnp.float32),
        "diffusivity": jnp.clip(jnp.exp(jax.random.uniform(key_of[1], (4,), jnp.float32, math.log(0.05), math.log(0.3))), 0.05, 0.3),
        "records": bell_draw(key_of[2], (6, PARTICLES), 1.0, 6.0, ((1, 32),), jnp.float32),
        "response_time": jnp.clip(jnp.exp(math.log(4.0) - 2.0794415 * jax.random.uniform(key_of[3], (PARTICLES,), jnp.float32) ** block_scale(key_of[3], (PARTICLES,), ((0, 32),), -0.2, 0.2)), 0.5, 4.0),
        "cell_index": place_ends(jax.random.randint(key_of[4], (PARTICLES,), 0, NX * YR * ZC), jax.random.fold_in(key_of[4], 1), 0, (NX * YR * ZC) - 1).astype(jnp.int32),
        "counts": draw_counts(jax.random.fold_in(key_of[8], 71), 0),
        "destination": draw_destination(jax.random.fold_in(key_of[8], 71), 0),
        "slot": draw_slot(jax.random.fold_in(key_of[8], 71), 0),
    }


time_step = 0.2
coupling = 0.5
stretch = 1.5

def periodic_compact(points):
    index = jnp.arange(points, dtype=jnp.int32)
    offset = (index[None, :] - index[:, None]) % points
    lhs = jnp.where(offset == 0, 1.0, 0.0) + jnp.where((offset == 1) | (offset == points - 1), 1.0 / 3.0, 0.0)
    rhs = jnp.where(offset == 1, 7.0 / 9.0, 0.0) - jnp.where(offset == points - 1, 7.0 / 9.0, 0.0)
    rhs = rhs + jnp.where(offset == 2, 1.0 / 36.0, 0.0) - jnp.where(offset == points - 2, 1.0 / 36.0, 0.0)
    factor = jnp.linalg.cholesky(lhs.astype(jnp.float32))
    return jax.scipy.linalg.cho_solve((factor, True), rhs.astype(jnp.float32))

def wall_compact(points):
    index = jnp.arange(points, dtype=jnp.int32)
    first = index == 0
    final = index == points - 1
    near = (index == 1) | (index == points - 2)
    lower = jnp.where(first, 0.0, jnp.where(final, 2.0, jnp.where(near, 0.25, 1.0 / 3.0))).astype(jnp.float32)
    upper = jnp.where(final, 0.0, jnp.where(first, 2.0, jnp.where(near, 0.25, 1.0 / 3.0))).astype(jnp.float32)
    middle = jnp.ones((points,), jnp.float32)
    offset = index[None, :] - index[:, None]
    inner = jnp.where(offset == 1, 7.0 / 9.0, 0.0) - jnp.where(offset == -1, 7.0 / 9.0, 0.0)
    inner = inner + jnp.where(offset == 2, 1.0 / 36.0, 0.0) - jnp.where(offset == -2, 1.0 / 36.0, 0.0)
    padde_rows = jnp.where(offset == 1, 0.75, 0.0) - jnp.where(offset == -1, 0.75, 0.0)
    top_row = jnp.where(offset == 0, -2.5, 0.0) + jnp.where(offset == 1, 2.0, 0.0) + jnp.where(offset == 2, 0.5, 0.0)
    end_row = jnp.where(offset == 0, 2.5, 0.0) - jnp.where(offset == -1, 2.0, 0.0) - jnp.where(offset == -2, 0.5, 0.0)
    rhs = jnp.where(first[:, None], top_row, jnp.where(final[:, None], end_row, jnp.where(near[:, None], padde_rows, inner)))
    solved = lax.linalg.tridiagonal_solve(lower, middle, upper, rhs.astype(jnp.float32))
    coord = -1.0 + 2.0 * index.astype(jnp.float32) / (points - 1)
    slope = stretch * (1.0 - jnp.tanh(stretch * coord) ** 2) / math.tanh(stretch)
    return solved / slope[:, None]

def spectral_matrix(points):
    index = jnp.arange(points, dtype=jnp.int32)
    offset = index[:, None] - index[None, :]
    parity = (1 - 2 * (offset % 2)).astype(jnp.float32)
    angle = math.pi * offset.astype(jnp.float32) / points
    safe_angle = jnp.where(offset == 0, 1.0, angle)
    value = math.pi / points * parity * jnp.cos(safe_angle) / jnp.sin(safe_angle)
    return jnp.where(offset == 0, 0.0, value).astype(jnp.float32)

def reference(fields, diffusivity, records, response_time, cell_index, counts, destination, slot):
    highest = lax.Precision.HIGHEST
    deriv_x = periodic_compact(NX)
    deriv_y = wall_compact(NY)
    deriv_z = spectral_matrix(NZ)
    second_x = jnp.dot(deriv_x, deriv_x, precision=highest)
    second_y = jnp.dot(deriv_y, deriv_y, precision=highest)
    second_z = jnp.dot(deriv_z, deriv_z, precision=highest)
    speed_u = fields[0]
    speed_v = fields[1]
    speed_w = fields[2]

    def component_tendency(operands):
        field, viscous = operands
        along_x = jnp.einsum('ij,yjz->yiz', deriv_x, field, precision=highest)
        curve_x = jnp.einsum('ij,yjz->yiz', second_x, field, precision=highest)
        along_y = jnp.einsum('ij,jxz->ixz', deriv_y, field, precision=highest)
        curve_y = jnp.einsum('ij,jxz->ixz', second_y, field, precision=highest)
        along_z = jnp.einsum('ij,yxj->yxi', deriv_z, field, precision=highest)
        curve_z = jnp.einsum('ij,yxj->yxi', second_z, field, precision=highest)
        partial_x = -speed_u * along_x + viscous * curve_x
        partial_y = -speed_v * along_y + viscous * curve_y
        partial_z = -speed_w * along_z + viscous * curve_z
        return partial_x + partial_y + partial_z
    summed = lax.map(component_tendency, (fields, diffusivity))
    pencils = PENCIL_ROWS * PENCIL_COLS
    total_slots = PART_DEV * pencils
    position = jnp.arange(total_slots, dtype=jnp.int32)
    pencil = position // PART_DEV
    local = position % PART_DEV
    pencil_row = pencil // PENCIL_COLS
    pencil_col = pencil % PENCIL_COLS
    plane_y = pencil_row * YR + cell_index // (NX * ZC)
    plane_x = cell_index // ZC % NX
    plane_z = pencil_col * ZC + cell_index % ZC
    live = local < counts[pencil]
    fluid = fields[0:3][:, plane_y, plane_x, plane_z]
    drag = (fluid - records[3:6]) / response_time
    velocity = records[3:6] + time_step * drag
    moved_pos = records[0:3] + time_step * velocity
    moved = jnp.concatenate([moved_pos, velocity], axis=0)
    force = jnp.where(live[None, :], -coupling * drag, 0.0)
    deposit = jnp.zeros((3, NY, NX, NZ), jnp.float32).at[:, plane_y, plane_x, plane_z].add(force)
    tendency = summed.at[0:3].add(deposit)
    staying = live & (destination == 0)
    kept = jnp.where(staying[None, :], moved, 0.0)
    leaving = live & (destination > 0)
    target = jnp.where(leaving, pencil * (4 * MIG) + (destination - 1) * MIG + slot, pencils * 4 * MIG)
    outgoing = jnp.zeros((6, pencils * 4 * MIG + 1), jnp.float32).at[:, target].add(jnp.where(leaving[None, :], moved, 0.0))
    outgoing = outgoing[:, :-1].reshape(6, PENCIL_ROWS, PENCIL_COLS, 4, MIG)
    from_lower = jnp.pad(outgoing[:, :-1, :, 0], ((0, 0), (1, 0), (0, 0), (0, 0)))
    from_upper = jnp.pad(outgoing[:, 1:, :, 1], ((0, 0), (0, 1), (0, 0), (0, 0)))
    from_left = jnp.roll(outgoing[:, :, :, 2], 1, axis=2)
    from_right = jnp.roll(outgoing[:, :, :, 3], -1, axis=2)
    arrivals = jnp.stack([from_lower, from_upper, from_left, from_right], axis=0)
    arrivals = arrivals.reshape(4, 6, pencils * MIG)
    return (tendency, kept, arrivals)
```

```python
import functools

import jax
import jax.numpy as jnp
import ml_dtypes
import numpy as np
from jax import lax
from jax.experimental import pallas as pl
from jax.experimental.pallas import tpu as pltpu
from jax.sharding import PartitionSpec as P

MIG = 256
LANES = 128
MIB = 1 << 20

time_step = 0.2
coupling = 0.5
stretch = 1.5


def periodic_compact(points):
    index = np.arange(points)
    offset = (index[None, :] - index[:, None]) % points
    lhs = (offset == 0) + ((offset == 1) | (offset == points - 1)) / 3.0
    rhs = 7.0 / 9.0 * ((offset == 1) * 1.0 - (offset == points - 1))
    rhs = rhs + ((offset == 2) * 1.0 - (offset == points - 2)) / 36.0
    return np.linalg.solve(lhs, rhs)


def wall_compact(points):
    lhs = np.eye(points)
    rhs = np.zeros((points, points))
    for row in range(points):
        if row == 0:
            lhs[0, 1] = 2.0
            rhs[0, :3] = (-2.5, 2.0, 0.5)
        elif row == points - 1:
            lhs[row, row - 1] = 2.0
            rhs[row, -3:] = (-0.5, -2.0, 2.5)
        elif row in (1, points - 2):
            lhs[row, [row - 1, row + 1]] = 0.25
            rhs[row, [row - 1, row + 1]] = (-0.75, 0.75)
        else:
            lhs[row, [row - 1, row + 1]] = 1.0 / 3.0
            rhs[row, [row - 2, row - 1, row + 1, row + 2]] = (-1 / 36, -7 / 9, 7 / 9, 1 / 36)
    coord = -1.0 + 2.0 * np.arange(points) / (points - 1)
    slope = stretch * (1.0 - np.tanh(stretch * coord) ** 2) / np.tanh(stretch)
    return np.linalg.solve(lhs, rhs) / slope[:, None]


def spectral_matrix(points):
    index = np.arange(points)
    offset = index[:, None] - index[None, :]
    parity = 1 - 2 * (offset % 2)
    angle = np.pi * np.where(offset == 0, 1, offset) / points
    return np.where(offset == 0, 0.0, np.pi / points * parity / np.tan(angle))


def two_terms(matrix):
    exact = np.asarray(matrix, np.float32)
    high = exact.astype(ml_dtypes.bfloat16)
    low = (exact - high.astype(np.float32)).astype(ml_dtypes.bfloat16)
    return high, low


def split(value, terms):
    pieces = []
    for _ in range(terms):
        piece = value.astype(jnp.bfloat16)
        pieces.append(piece)
        value = value - piece.astype(jnp.float32)
    return pieces


def dot(a, b):
    return lax.dot_general(a, b, (((1,), (0,)), ((), ())), preferred_element_type=jnp.float32)


def dot_transposed(a, b):
    return lax.dot_general(a, b, (((1,), (1,)), ((), ())), preferred_element_type=jnp.float32)


def one_hot(mask):
    return jnp.where(mask, 1.0, 0.0).astype(jnp.bfloat16)


def sublane_iota(rows, columns):
    return lax.broadcasted_iota(jnp.int32, (rows, columns), 0)


def params(mib):
    return pltpu.CompilerParams(vmem_limit_bytes=mib * MIB)


def cost(flops, nbytes):
    return pl.CostEstimate(flops=int(flops), bytes_accessed=int(nbytes), transcendentals=0)


def any_space(shape):
    return jax.ShapeDtypeStruct(tuple(shape), jnp.float32)


VMEM = pl.BlockSpec(memory_space=pltpu.VMEM)
SMEM = pl.BlockSpec(memory_space=pltpu.SMEM)


def advance_kernel(chunk, count_ref, fields_ref, records_ref, response_ref, cell_ref, destination_ref, slot_ref,
                   kept_ref, force_ref, outgoing_ref, table_ref, total_ref):
    planes, width, lanes = fields_ref.shape[1:]
    rows = planes * width
    particles = records_ref.shape[1]
    for component in range(3):
        plane = fields_ref[component].reshape(rows, lanes).T
        high, low = split(plane, 2)
        table_ref[component * lanes:(component + 1) * lanes, :rows] = high
        table_ref[component * lanes:(component + 1) * lanes, rows:] = low
    total_ref[...] = jnp.zeros_like(total_ref)
    groups = 4 * MIG // LANES

    def step(index, carry):
        start = pl.multiple_of(index * chunk, chunk)
        window = pl.ds(start, chunk)
        cell = cell_ref[:, window]
        row_hot = one_hot(sublane_iota(rows, chunk) == cell // lanes)
        found = dot(table_ref[...], jnp.concatenate([row_hot, row_hot], axis=0))
        at_lane = sublane_iota(lanes, chunk) == cell % lanes
        fluid = jnp.concatenate(
            [jnp.sum(jnp.where(at_lane, found[a * lanes:(a + 1) * lanes], 0.0), axis=0, keepdims=True) for a in range(3)],
            axis=0)
        records = records_ref[:, window]
        speed = records[3:6]
        drag = (fluid - speed) / response_ref[:, window]
        velocity = speed + time_step * drag
        moved = jnp.concatenate([records[0:3] + time_step * velocity, velocity], axis=0)
        live = start + lax.broadcasted_iota(jnp.int32, (1, chunk), 1) < count_ref[0]
        destination = destination_ref[:, window]
        kept_ref[:, window] = jnp.where(live & (destination == 0), moved, 0.0)
        force_ref[:, window] = jnp.where(live, -coupling * drag, 0.0)
        target = jnp.where(live & (destination > 0), (destination - 1) * MIG + slot_ref[:, window], -1)
        in_group = sublane_iota(groups, chunk) == target // LANES
        slot_hot = one_hot(sublane_iota(LANES, chunk) == target % LANES)
        pieces = []
        rest = moved
        for _ in range(3):
            piece = rest.astype(jnp.bfloat16).astype(jnp.float32)
            rest = rest - piece
            pieces += [jnp.where(in_group, piece[a:a + 1], 0.0) for a in range(6)]
        sent = jnp.concatenate(pieces, axis=0).astype(jnp.bfloat16)
        total_ref[...] += dot_transposed(sent, slot_hot)
        return carry

    lax.fori_loop(0, particles // chunk, step, 0)
    total = total_ref[...].reshape(3, 6, groups, LANES)
    outgoing_ref[...] = total[0] + total[1] + total[2]


def advance(counts, fields, records, response, cell, destination, slot):
    planes, width, lanes = fields.shape[1:]
    rows = planes * width
    particles = records.shape[1]
    chunk = min(1024 if rows <= 256 else 256, particles)
    groups = 4 * MIG // LANES
    return pl.pallas_call(
        functools.partial(advance_kernel, chunk),
        out_shape=(any_space((6, particles)), any_space((3, particles)), any_space((6, groups, LANES))),
        in_specs=[SMEM] + [VMEM] * 6,
        out_specs=(VMEM,) * 3,
        scratch_shapes=[pltpu.VMEM((3 * lanes, 2 * rows), jnp.bfloat16), pltpu.VMEM((18 * groups, LANES), jnp.float32)],
        compiler_params=params(32),
        cost_estimate=cost(2 * 3 * lanes * 2 * rows * particles, 4 * 20 * particles + fields.size * 4),
        name="advance",
    )(counts, fields, records, response, cell, destination, slot)


def along_x_kernel(chunk, viscous_ref, fields_ref, operator_ref, cell_ref, force_ref, out_ref, total_ref):
    parts, planes, width, lanes = fields_ref.shape
    rows = planes * width
    half = rows // 2
    particles = cell_ref.shape[1]
    total_ref[...] = jnp.zeros_like(total_ref)

    def step(index, carry):
        window = pl.ds(pl.multiple_of(index * chunk, chunk), chunk)
        cell = cell_ref[:, window]
        row = cell // lanes
        column = jnp.where(row >= half, lanes, 0) + cell % lanes
        at_row = sublane_iota(half, chunk) == row % half
        column_hot = one_hot(sublane_iota(2 * lanes, chunk) == column)
        pieces = []
        force = force_ref[:, window]
        for _ in range(2):
            piece = force.astype(jnp.bfloat16).astype(jnp.float32)
            force = force - piece
            pieces += [jnp.where(at_row, piece[a:a + 1], 0.0).astype(jnp.bfloat16) for a in range(3)]
        total_ref[...] += dot_transposed(jnp.concatenate(pieces, axis=0), column_hot)
        return carry

    lax.fori_loop(0, particles // chunk, step, 0)
    for component in range(parts):
        viscous = viscous_ref[component]
        for plane in range(planes):
            field = fields_ref[component, plane]
            high, low = split(field, 2)
            stacked = jnp.concatenate([high, low, high], axis=0)
            both = dot(operator_ref[...], stacked)
            value = -fields_ref[0, plane] * both[:width] + viscous * both[width:]
            if component < 3:
                for start in range(plane * width, (plane + 1) * width, min(width, half)):
                    part, first = divmod(start, half)
                    size = min(width, half)
                    columns = slice(part * lanes, (part + 1) * lanes)
                    base = component * half + first
                    deposit = (total_ref[base:base + size, columns]
                               + total_ref[3 * half + base:3 * half + base + size, columns])
                    inside = start - plane * width
                    out_ref[component, plane, inside:inside + size] = value[inside:inside + size] + deposit
            else:
                out_ref[component, plane] = value


def along_x(viscous, fields, cell, force):
    parts, planes, width, lanes = fields.shape
    half = planes * width // 2
    particles = cell.shape[1]
    chunk = min(1024 if half <= 128 else 256, particles)
    deriv = periodic_compact(width)
    high, low = two_terms(np.concatenate([deriv, deriv @ deriv], axis=0))
    operator = jnp.asarray(np.concatenate([high, high, low], axis=1))
    return pl.pallas_call(
        functools.partial(along_x_kernel, chunk),
        out_shape=any_space(fields.shape),
        in_specs=[SMEM] + [VMEM] * 4,
        out_specs=VMEM,
        scratch_shapes=[pltpu.VMEM((6 * half, 2 * lanes), jnp.float32)],
        compiler_params=params(40),
        cost_estimate=cost(2 * 6 * half * 2 * lanes * particles, fields.size * 8 + 16 * particles),
        name="along_x",
    )(viscous, fields, operator, cell, force)


def along_z_kernel(viscous_ref, high_ref, low_ref, *refs):
    count = len(refs) // 2
    blocks, results = refs[:count], refs[count:]
    parts, planes, width, lanes = blocks[0].shape
    rows = parts * planes * width
    pieces = [split(block[...].reshape(rows, lanes), 2) for block in blocks]

    def lines(term):
        return jnp.concatenate(
            [jnp.concatenate([pieces[(d - s) % count][term] for d in range(count)], axis=1) for s in range(count)], axis=0)

    high = lines(0)
    both = dot(high, high_ref[...]) + dot(lines(1), high_ref[...]) + dot(high, low_ref[...])
    for s in range(count):
        speed = blocks[(-s) % count][2]
        for component in range(parts):
            first = s * rows + component * planes * width
            part = both[first:first + planes * width]
            along = part[:, :lanes].reshape(planes, width, lanes)
            curve = part[:, lanes:].reshape(planes, width, lanes)
            results[s][component] = -speed * along + viscous_ref[component] * curve


def along_z(viscous, blocks):
    count = len(blocks)
    shape = blocks[0].shape
    lanes = shape[3]
    points = count * lanes
    deriv = spectral_matrix(points)
    second = deriv @ deriv
    weights = [
        np.concatenate([matrix[d * lanes:(d + 1) * lanes, :lanes].T for matrix in (deriv, second)], axis=1)
        for d in range(count)
    ]
    high, low = two_terms(np.concatenate(weights, axis=0))
    size = int(np.prod(shape))
    return pl.pallas_call(
        along_z_kernel,
        out_shape=tuple(any_space(shape) for _ in blocks),
        in_specs=[SMEM] + [VMEM] * (2 + count),
        out_specs=(VMEM,) * count,
        compiler_params=params(48),
        cost_estimate=cost(2 * 3 * size * count * points * 2, 8 * count * size),
        name="along_z",
    )(viscous, jnp.asarray(high), jnp.asarray(low), *blocks)


def along_y_kernel(viscous_ref, weight_ref, *refs):
    blocks, out_ref = refs[:-1], refs[-1]
    parts, planes, width, lanes = out_ref.shape
    for component in range(parts):
        viscous = viscous_ref[component]
        along = [jnp.zeros((width, lanes), jnp.float32) for _ in range(planes)]
        curve = [jnp.zeros((width, lanes), jnp.float32) for _ in range(planes)]
        for s, block in enumerate(blocks):
            for source in range(planes):
                value = block[component, source]
                for plane in range(planes):
                    base = ((s * planes + source) * planes + plane) * 2
                    along[plane] += weight_ref[base] * value
                    curve[plane] += weight_ref[base + 1] * value
        for plane in range(planes):
            out_ref[component, plane] = -blocks[0][1, plane] * along[plane] + viscous * curve[plane]


def along_y(viscous, blocks):
    count = len(blocks)
    planes = blocks[0].shape[1]
    deriv = wall_compact(count * planes)
    second = deriv @ deriv
    table = np.zeros((count, count, planes, planes, 2), np.float32)
    for me in range(count):
        for s in range(count):
            for source in range(planes):
                for plane in range(planes):
                    place = (me * planes + plane, (me ^ s) * planes + source)
                    table[me, s, source, plane] = deriv[place], second[place]
    weights = lax.dynamic_index_in_dim(jnp.asarray(table.reshape(count, -1)), lax.axis_index("row"), 0, keepdims=False)
    size = blocks[0].size
    return pl.pallas_call(
        along_y_kernel,
        out_shape=any_space(blocks[0].shape),
        in_specs=[SMEM, SMEM] + [VMEM] * count,
        out_specs=VMEM,
        compiler_params=params(32),
        cost_estimate=cost(4 * size * count * planes, 4 * size * (count + 1)),
        name="along_y",
    )(viscous, weights, *blocks)


def gathered_lines(fields):
    count = lax.axis_size("row")
    blocks = {0: fields}
    for s in range(2, count, 2):
        blocks[s] = lax.ppermute(fields, "row", [(i, i ^ s) for i in range(count)])
    for s in range(0, count, 2):
        blocks[s + 1] = lax.ppermute(blocks[s], "row", [(i, i ^ 1) for i in range(count)])
    return [blocks[s] for s in range(count)]


def pencil_along_y(viscous, fields):
    highest = lax.Precision.HIGHEST
    pencil = lax.all_to_all(fields, "row", split_axis=2, concat_axis=1, tiled=True)
    deriv = wall_compact(pencil.shape[1])
    operators = [jnp.asarray(matrix, jnp.float32) for matrix in (deriv, deriv @ deriv)]
    along, curve = (jnp.einsum("ij,cjxz->cixz", matrix, pencil, precision=highest) for matrix in operators)
    partial = -pencil[1] * along + viscous[:, None, None, None] * curve
    return lax.all_to_all(partial, "row", split_axis=1, concat_axis=2, tiled=True)


def total_kernel(place_ref, *refs):
    along_x_ref, along_y_ref = refs[:2]
    blocks, out_ref = refs[2:-1], refs[-1]
    count = len(blocks)
    width = blocks[0].shape[2]
    for s, block in enumerate(blocks):
        rows = pl.ds(pl.multiple_of(lax.rem(place_ref[0] + count - s, count) * width, width), width)
        out_ref[:, :, rows, :] = along_x_ref[:, :, rows, :] + along_y_ref[:, :, rows, :] + block[...]


def total(place, along_x_part, along_y_part, blocks):
    size = along_x_part.size
    return pl.pallas_call(
        total_kernel,
        out_shape=any_space(along_x_part.shape),
        in_specs=[SMEM] + [VMEM] * (2 + len(blocks)),
        out_specs=VMEM,
        compiler_params=params(32),
        cost_estimate=cost(3 * size, 16 * size),
        name="total",
    )(place, along_x_part, along_y_part, *blocks)


def exchange(blocks):
    count = lax.axis_size("col")
    received = list(blocks)
    for s in sorted(range(1, count), key=lambda s: -min(s, count - s)):
        received[s] = lax.ppermute(blocks[s], "col", [(i, (i + s) % count) for i in range(count)])
    return received


def on_device(fields, diffusivity, records, response_time, cell_index, counts, destination, slot):
    columns = lax.axis_size("col")
    place = lax.axis_index("col")
    width = fields.shape[2] // columns
    response = response_time.reshape(1, -1)
    cell = cell_index.reshape(1, -1)
    blocks = [
        lax.dynamic_slice_in_dim(fields, (place + s) % columns * width, width, axis=2) for s in range(columns)
    ]
    lines = exchange(blocks)
    kept, force, outgoing = advance(
        counts, fields, records, response, cell, destination.reshape(1, -1), slot.reshape(1, -1))
    outgoing = outgoing.reshape(6, 4, MIG)
    terms_z = exchange(along_z(diffusivity, lines))
    rows = lax.axis_size("row")
    if rows & (rows - 1) == 0 and rows * fields.size * 4 <= 16 * MIB:
        terms_y = along_y(diffusivity, gathered_lines(fields))
    else:
        terms_y = pencil_along_y(diffusivity, fields)
    terms_x = along_x(diffusivity, fields, cell, force)
    tendency = total(place.reshape(1), terms_x, terms_y, terms_z)
    steps = [(i, i + 1) for i in range(rows - 1)]
    ring = [(i, (i + 1) % columns) for i in range(columns)]
    arrivals = jnp.stack(
        [
            lax.ppermute(outgoing[:, 0], "row", steps),
            lax.ppermute(outgoing[:, 1], "row", [(b, a) for a, b in steps]),
            lax.ppermute(outgoing[:, 2], "col", ring),
            lax.ppermute(outgoing[:, 3], "col", [(b, a) for a, b in ring]),
        ],
        axis=0,
    )
    return (tendency, kept, arrivals)


def solution(mesh):
    return jax.shard_map(
        on_device,
        mesh=mesh,
        in_specs=(
            P(None, "row", None, "col"),
            P(),
            P(None, ("row", "col")),
            P(("row", "col")),
            P(("row", "col")),
            P(("row", "col")),
            P(("row", "col")),
            P(("row", "col")),
        ),
        out_specs=(
            P(None, "row", None, "col"),
            P(None, ("row", "col")),
            P(None, None, ("row", "col")),
        ),
        check_vma=False,
    )
```

```python
import functools

import jax
import jax.numpy as jnp
import ml_dtypes
import numpy as np
from jax import lax
from jax.experimental import pallas as pl
from jax.experimental.pallas import tpu as pltpu
from jax.sharding import PartitionSpec as P

MIG = 256
LANES = 128
MIB = 1 << 20

time_step = 0.2
coupling = 0.5
stretch = 1.5


def periodic_compact(points):
    index = np.arange(points)
    offset = (index[None, :] - index[:, None]) % points
    lhs = (offset == 0) + ((offset == 1) | (offset == points - 1)) / 3.0
    rhs = 7.0 / 9.0 * ((offset == 1) * 1.0 - (offset == points - 1))
    rhs = rhs + ((offset == 2) * 1.0 - (offset == points - 2)) / 36.0
    return np.linalg.solve(lhs, rhs)


def wall_compact(points):
    lhs = np.eye(points)
    rhs = np.zeros((points, points))
    for row in range(points):
        if row == 0:
            lhs[0, 1] = 2.0
            rhs[0, :3] = (-2.5, 2.0, 0.5)
        elif row == points - 1:
            lhs[row, row - 1] = 2.0
            rhs[row, -3:] = (-0.5, -2.0, 2.5)
        elif row in (1, points - 2):
            lhs[row, [row - 1, row + 1]] = 0.25
            rhs[row, [row - 1, row + 1]] = (-0.75, 0.75)
        else:
            lhs[row, [row - 1, row + 1]] = 1.0 / 3.0
            rhs[row, [row - 2, row - 1, row + 1, row + 2]] = (-1 / 36, -7 / 9, 7 / 9, 1 / 36)
    coord = -1.0 + 2.0 * np.arange(points) / (points - 1)
    slope = stretch * (1.0 - np.tanh(stretch * coord) ** 2) / np.tanh(stretch)
    return np.linalg.solve(lhs, rhs) / slope[:, None]


def spectral_matrix(points):
    index = np.arange(points)
    offset = index[:, None] - index[None, :]
    parity = 1 - 2 * (offset % 2)
    angle = np.pi * np.where(offset == 0, 1, offset) / points
    return np.where(offset == 0, 0.0, np.pi / points * parity / np.tan(angle))


def two_terms(matrix):
    exact = np.asarray(matrix, np.float32)
    high = exact.astype(ml_dtypes.bfloat16)
    low = (exact - high.astype(np.float32)).astype(ml_dtypes.bfloat16)
    return high, low


def split(value, terms):
    pieces = []
    for _ in range(terms):
        piece = value.astype(jnp.bfloat16)
        pieces.append(piece)
        value = value - piece.astype(jnp.float32)
    return pieces


def dot(a, b):
    return lax.dot_general(a, b, (((1,), (0,)), ((), ())), preferred_element_type=jnp.float32)


def dot_transposed(a, b):
    return lax.dot_general(a, b, (((1,), (1,)), ((), ())), preferred_element_type=jnp.float32)


def sublane_iota(rows, columns, dtype=jnp.int32):
    return lax.broadcasted_iota(dtype, (rows, columns), 0)


def is_row(rows, index):
    return sublane_iota(rows, index.shape[1], jnp.int16) == index.astype(jnp.int16)


def one_hot(rows, index):
    return jnp.where(is_row(rows, index), jnp.bfloat16(1), jnp.bfloat16(0))


def chunk_of(particles, rows):
    chunk = particles
    while chunk * rows > 1 << 20 and chunk % 256 == 0:
        chunk //= 2
    return chunk


def params(mib):
    return pltpu.CompilerParams(vmem_limit_bytes=mib * MIB)


CHEAP = pl.CostEstimate(flops=1, bytes_accessed=1, transcendentals=0)


def any_space(shape):
    return jax.ShapeDtypeStruct(tuple(shape), jnp.float32)


VMEM = pl.BlockSpec(memory_space=pltpu.VMEM)
SMEM = pl.BlockSpec(memory_space=pltpu.SMEM)


def advance_kernel(chunk, place_ref, count_ref, fields_ref, records_ref, response_ref, cell_ref, destination_ref,
                   slot_ref, kept_ref, force_ref, near_ref, side_ref, payload_ref, table_ref, total_ref):
    planes, width, lanes = fields_ref.shape[1:]
    rows = planes * width
    particles = records_ref.shape[1]
    for component in range(3):
        plane = fields_ref[component].reshape(rows, lanes).T
        high, low = split(plane, 2)
        table_ref[component * lanes:(component + 1) * lanes, :rows] = high
        table_ref[component * lanes:(component + 1) * lanes, rows:] = low
    groups = 4 * MIG // LANES

    def step(index, sums):
        window = pl.ds(index * chunk, chunk)
        cell = cell_ref[:, window]
        row_hot = one_hot(rows, cell // lanes)
        found = dot(table_ref[...], jnp.concatenate([row_hot, row_hot], axis=0))
        at_lane = sublane_iota(lanes, chunk) == cell % lanes
        fluid = jnp.concatenate(
            [jnp.sum(jnp.where(at_lane, found[a * lanes:(a + 1) * lanes], 0.0), axis=0, keepdims=True) for a in range(3)],
            axis=0)
        records = records_ref[:, window]
        speed = records[3:6]
        drag = (fluid - speed) / response_ref[:, window]
        velocity = speed + time_step * drag
        moved = jnp.concatenate([records[0:3] + time_step * velocity, velocity], axis=0)
        live = index * chunk + lax.broadcasted_iota(jnp.int32, (1, chunk), 1) < count_ref[0]
        destination = destination_ref[:, window]
        kept_ref[:, window] = jnp.where(live & (destination == 0), moved, 0.0)
        force_ref[:, window] = jnp.where(live, -coupling * drag, 0.0)
        target = jnp.where(live & (destination > 0), (destination - 1) * MIG + slot_ref[:, window], -LANES)
        group = target // LANES
        slot_hot = one_hot(LANES, target % LANES)
        padded = jnp.concatenate([moved, jnp.zeros((2, chunk), jnp.float32)], axis=0)
        pieces = []
        for _ in range(2):
            piece = padded.astype(jnp.bfloat16).astype(jnp.float32)
            padded = padded - piece
            pieces += [jnp.where(group == g, piece, 0.0) for g in range(groups)]
        sent = jnp.concatenate(pieces, axis=0).astype(jnp.bfloat16)
        return sums + dot_transposed(sent, slot_hot)

    total_ref[...] = jnp.zeros_like(total_ref)
    if chunk == particles:
        total_ref[...] = step(0, total_ref[...])
    else:
        def loop(index, carry):
            total_ref[...] = step(pl.multiple_of(index, 1), total_ref[...])
            return carry

        lax.fori_loop(0, particles // chunk, loop, 0)
    outgoing = (total_ref[:8 * groups] + total_ref[8 * groups:]).reshape(4, groups // 4, 8, LANES)
    even = lax.rem(place_ref[0], 2) == 0
    near_ref[...] = jnp.where(even, outgoing[0], outgoing[1])
    side_ref[...] = outgoing[2:]
    size = fields_ref.shape[0] * rows
    payload_ref[:size] = fields_ref[...].reshape(size, lanes)
    payload_ref[size:] = jnp.where(even, outgoing[1], outgoing[0]).reshape(-1, LANES)


def advance(place, counts, fields, records, response, cell, destination, slot):
    planes, width, lanes = fields.shape[1:]
    rows = planes * width
    particles = records.shape[1]
    groups = 4 * MIG // LANES
    box = (groups // 4, 8, LANES)
    payload = (fields.size // lanes + groups // 4 * 8, lanes)
    return pl.pallas_call(
        functools.partial(advance_kernel, chunk_of(particles, rows)),
        out_shape=(any_space((6, particles)), any_space((3, particles)), any_space(box), any_space((2, *box)), any_space(payload)),
        in_specs=[SMEM] * 2 + [VMEM] * 6,
        out_specs=(VMEM,) * 5,
        scratch_shapes=[pltpu.VMEM((3 * lanes, 2 * rows), jnp.bfloat16), pltpu.VMEM((16 * groups, LANES), jnp.float32)],
        compiler_params=params(40),
        cost_estimate=CHEAP,
        name="advance",
    )(place, counts, fields, records, response, cell, destination, slot)


def along_x_kernel(chunk, viscous_ref, fields_ref, operator_ref, cell_ref, force_ref, out_ref, total_ref):
    parts, planes, width, lanes = fields_ref.shape
    rows = planes * width
    half = rows // 2
    particles = cell_ref.shape[1]
    total_ref[...] = jnp.zeros_like(total_ref)

    def step(index):
        window = pl.ds(index * chunk, chunk)
        cell = cell_ref[:, window]
        row = cell // lanes
        column = jnp.where(row >= half, lanes, 0) + cell % lanes
        at_row = is_row(half, row % half)
        column_hot = one_hot(2 * lanes, column)
        pieces = []
        force = force_ref[:, window]
        for _ in range(2):
            piece = force.astype(jnp.bfloat16)
            force = force - piece.astype(jnp.float32)
            pieces += [jnp.where(at_row, piece[a:a + 1], jnp.bfloat16(0)) for a in range(3)]
        return dot_transposed(jnp.concatenate(pieces, axis=0), column_hot)

    if chunk == particles:
        total_ref[...] = step(0)
    else:
        def loop(index, carry):
            total_ref[...] += step(index)
            return carry

        lax.fori_loop(0, particles // chunk, loop, 0)
    for component in range(parts):
        viscous = viscous_ref[component]
        for plane in range(planes):
            field = fields_ref[component, plane]
            high, low = split(field, 2)
            stacked = jnp.concatenate([high, low, high], axis=0)
            both = dot(operator_ref[...], stacked)
            value = -fields_ref[0, plane] * both[:width] + viscous * both[width:]
            if component < 3:
                for start in range(plane * width, (plane + 1) * width, min(width, half)):
                    part, first = divmod(start, half)
                    size = min(width, half)
                    columns = slice(part * lanes, (part + 1) * lanes)
                    base = component * half + first
                    deposit = (total_ref[base:base + size, columns]
                               + total_ref[3 * half + base:3 * half + base + size, columns])
                    inside = start - plane * width
                    out_ref[component, plane, inside:inside + size] = value[inside:inside + size] + deposit
            else:
                out_ref[component, plane] = value


def along_x(viscous, fields, cell, force):
    parts, planes, width, lanes = fields.shape
    half = planes * width // 2
    particles = cell.shape[1]
    deriv = periodic_compact(width)
    high, low = two_terms(np.concatenate([deriv, deriv @ deriv], axis=0))
    operator = jnp.asarray(np.concatenate([high, high, low], axis=1))
    return pl.pallas_call(
        functools.partial(along_x_kernel, chunk_of(particles, 2 * half)),
        out_shape=any_space(fields.shape),
        in_specs=[SMEM] + [VMEM] * 4,
        out_specs=VMEM,
        scratch_shapes=[pltpu.VMEM((6 * half, 2 * lanes), jnp.float32)],
        compiler_params=params(40),
        cost_estimate=CHEAP,
        name="along_x",
    )(viscous, fields, operator, cell, force)


def along_z_kernel(viscous_ref, high_ref, low_ref, side_ref, *refs):
    count = len(refs) // 2
    blocks, results = refs[:count], refs[count:]
    parts, planes, width, lanes = blocks[0].shape
    rows = parts * planes * width
    pieces = [split(block[...].reshape(rows, lanes), 2) for block in blocks]

    def lines(term):
        return jnp.concatenate(
            [jnp.concatenate([pieces[(d - s) % count][term] for d in range(count)], axis=1) for s in range(count)], axis=0)

    high = lines(0)
    both = dot(high, high_ref[...]) + dot(lines(1), high_ref[...]) + dot(high, low_ref[...])
    for s in range(count):
        speed = blocks[(-s) % count][2]
        for component in range(parts):
            first = s * rows + component * planes * width
            part = both[first:first + planes * width]
            along = part[:, :lanes].reshape(planes, width, lanes)
            curve = part[:, lanes:].reshape(planes, width, lanes)
            value = -speed * along + viscous_ref[component] * curve
            results[s][component * planes * width:(component + 1) * planes * width] = value.reshape(planes * width, lanes)
        row = rows
        for direction in riding(s, count):
            for group in range(side_ref.shape[1]):
                results[s][row:row + 8] = side_ref[direction - 2, group]
                row += 8


def riding(s, count):
    return [direction for direction, step in ((2, 1), (3, -1)) if s == step % count]


def along_z(viscous, side, blocks):
    count = len(blocks)
    shape = blocks[0].shape
    lanes = shape[3]
    points = count * lanes
    deriv = spectral_matrix(points)
    second = deriv @ deriv
    weights = [
        np.concatenate([matrix[d * lanes:(d + 1) * lanes, :lanes].T for matrix in (deriv, second)], axis=1)
        for d in range(count)
    ]
    high, low = two_terms(np.concatenate(weights, axis=0))
    size = int(np.prod(shape))
    return pl.pallas_call(
        along_z_kernel,
        out_shape=tuple(any_space((size // lanes + MIG // LANES * 8 * len(riding(s, count)), lanes)) for s in range(count)),
        in_specs=[SMEM] + [VMEM] * (3 + count),
        out_specs=(VMEM,) * count,
        compiler_params=params(48),
        cost_estimate=CHEAP,
        name="along_z",
    )(viscous, jnp.asarray(high), jnp.asarray(low), side, *blocks)


def along_y_kernel(place_ref, weight_ref, near_ref, fields_ref, *refs):
    others, (own_ref, sibling_ref) = refs[:-2], refs[-2:]
    parts, planes, width, lanes = fields_ref.shape
    count = 2 * (len(others) + 1)
    size = parts * planes * width
    mine = place_ref[0] * (count * planes * planes * 2)
    step = min(width, 32)
    for component in range(parts):
        for first in range(0, width, step):
            sums = [[None] * 2 for _ in range(2 * planes)]
            for index in range(count // 2):
                for source in range(planes):
                    if index == 0:
                        value = fields_ref[component, source, first:first + step]
                    else:
                        row = (component * planes + source) * width + first
                        value = others[index - 1][row:row + step]
                    for target in range(2 * planes):
                        for kind in range(2):
                            weight = weight_ref[mine + ((index * planes + source) * 2 * planes + target) * 2 + kind]
                            before = sums[target][kind]
                            sums[target][kind] = weight * value if before is None else before + weight * value
            for plane in range(planes):
                for kind in range(2):
                    row = kind * size + (component * planes + plane) * width + first
                    own_ref[row:row + step] = sums[plane][kind]
                    sibling_ref[row:row + step] = sums[planes + plane][kind]
    extra = MIG // LANES * 8
    sibling_ref[2 * size:2 * size + extra] = near_ref[...].reshape(extra, lanes)
    me = place_ref[0]
    sibling = me ^ 1
    origin = jnp.where(lax.rem(sibling, 2) == 0, sibling - 1, sibling + 1)
    passed = jnp.zeros((extra, lanes), jnp.float32)
    for index, other in enumerate(others):
        if other.shape[0] > size:
            here = (origin >= 0) & (origin < count) & ((origin ^ me) == 2 * index + 2)
            passed = jnp.where(here, other[size:], passed)
    sibling_ref[2 * size + extra:] = passed


def carries_particles(s):
    return (s + 2) & (s + 1) == 0


def early_y(fields):
    rows = lax.axis_size("row")
    block = fields.reshape(-1, fields.shape[3])
    return {
        s: lax.ppermute(block, "row", [(i, i ^ s) for i in range(rows)])
        for s in range(2, rows, 2) if not carries_particles(s)
    }


def along_y(place, near, fields, payload, others, after):
    rows = lax.axis_size("row")
    planes = fields.shape[1]
    deriv = wall_compact(rows * planes)
    operators = np.stack([deriv, deriv @ deriv], axis=-1)
    table = np.zeros((rows, rows // 2, planes, 2, planes, 2), np.float32)
    for me in range(rows):
        for index in range(rows // 2):
            for side in range(2):
                target, source = (me ^ side) * planes, (me ^ (2 * index)) * planes
                block = operators[target:target + planes, source:source + planes]
                table[me, index, :, side] = block.transpose(1, 0, 2)
    for s in range(2, rows, 2):
        if carries_particles(s):
            others[s] = lax.ppermute(payload, "row", [(i, i ^ s) for i in range(rows)])
    others = [others[s] for s in range(2, rows, 2)]
    *others, _ = lax.optimization_barrier((*others, after))
    size = fields.size // fields.shape[3]
    own, sibling = pl.pallas_call(
        along_y_kernel,
        out_shape=(any_space((2 * size, LANES)), any_space((2 * size + MIG // LANES * 16, LANES))),
        in_specs=[SMEM] * 2 + [VMEM] * (2 + len(others)),
        out_specs=(VMEM, VMEM),
        compiler_params=params(32),
        cost_estimate=CHEAP,
        name="along_y",
    )(place, jnp.asarray(table.reshape(-1)), near, fields, *others)
    return own, lax.ppermute(sibling, "row", [(i, i ^ 1) for i in range(rows)])


def pencil_along_y(viscous, fields):
    highest = lax.Precision.HIGHEST
    pencil = lax.all_to_all(fields, "row", split_axis=2, concat_axis=1, tiled=True)
    deriv = wall_compact(pencil.shape[1])
    operators = [jnp.asarray(matrix, jnp.float32) for matrix in (deriv, deriv @ deriv)]
    along, curve = (jnp.einsum("ij,cjxz->cixz", matrix, pencil, precision=highest) for matrix in operators)
    partial = -pencil[1] * along + viscous[:, None, None, None] * curve
    return lax.all_to_all(partial, "row", split_axis=1, concat_axis=2, tiled=True)


def total_kernel(gathered, place_ref, viscous_ref, along_x_ref, *refs):
    own, refs = refs[:3] if gathered else refs[:2], refs[3:] if gathered else refs[2:]
    blocks, out_ref, arrivals_ref = refs[:-2], refs[-2], refs[-1]
    count = len(blocks)
    parts, planes, width, lanes = out_ref.shape
    size = width // count
    whole = parts * planes * width
    for s, block in enumerate(blocks):
        start = pl.multiple_of(lax.rem(place_ref[1] + count - s, count) * size, size)
        rows = pl.ds(start, size)
        for component in range(parts):
            for plane in range(planes):
                first = (component * planes + plane) * size
                value = along_x_ref[component, plane, rows, :] + block[first:first + size]
                if gathered:
                    fields_ref, own_ref, sibling_ref = own
                    row = pl.multiple_of((component * planes + plane) * width + start, size)
                    near, far = pl.ds(row, size), pl.ds(whole + row, size)
                    along = own_ref[near] + sibling_ref[near]
                    curve = own_ref[far] + sibling_ref[far]
                    value += viscous_ref[component] * curve - fields_ref[1, plane, rows, :] * along
                out_ref[component, plane, rows, :] = value
        first = parts * planes * size
        for direction in riding(s, count):
            for group in range(MIG // LANES):
                columns = slice(group * LANES, (group + 1) * LANES)
                arrivals_ref[:, direction, columns] = block[first:first + 6]
                first += 8
    even = lax.rem(place_ref[0], 2) == 0
    extra = MIG // LANES * 8
    for group in range(MIG // LANES):
        columns = slice(group * LANES, (group + 1) * LANES)
        if gathered:
            near = own[2][2 * whole + group * 8:2 * whole + group * 8 + 6]
            far = own[2][2 * whole + extra + group * 8:2 * whole + extra + group * 8 + 6]
        else:
            near, far = own[0][group, :6], own[1][group * 8:group * 8 + 6]
        arrivals_ref[:, 0, columns] = jnp.where(even, far, near)
        arrivals_ref[:, 1, columns] = jnp.where(even, near, far)


def total(gathered, place, viscous, along_x_part, own, blocks):
    size = along_x_part.size
    return pl.pallas_call(
        functools.partial(total_kernel, gathered),
        out_shape=(any_space(along_x_part.shape), any_space((6, 4, MIG))),
        in_specs=[SMEM] * 2 + [VMEM] * (1 + len(own) + len(blocks)),
        out_specs=(VMEM, VMEM),
        compiler_params=params(32),
        cost_estimate=CHEAP,
        name="total",
    )(place, viscous, along_x_part, *own, *blocks)


def exchange(blocks):
    count = lax.axis_size("col")
    received = list(blocks)
    for s in sorted(range(1, count), key=lambda s: -min(s, count - s)):
        received[s] = lax.ppermute(blocks[s], "col", [(i, (i + s) % count) for i in range(count)])
    return received


def on_device(fields, diffusivity, records, response_time, cell_index, counts, destination, slot):
    rows, columns = lax.axis_size("row"), lax.axis_size("col")
    column = lax.axis_index("col")
    place = jnp.stack([lax.axis_index("row"), column])
    width = fields.shape[2] // columns
    cell = cell_index.reshape(1, -1)
    blocks = [
        lax.dynamic_slice_in_dim(fields, (column + s) % columns * width, width, axis=2) for s in range(columns)
    ]
    lines = exchange(blocks)
    kept, force, near, side, payload = advance(
        place, counts, fields, records, response_time.reshape(1, -1), cell, destination.reshape(1, -1),
        slot.reshape(1, -1))
    others = early_y(fields)
    payload, side, lines, others = lax.optimization_barrier((payload, side, lines, others))
    terms_z = along_z(diffusivity, side, lines)
    force, *terms_z = lax.optimization_barrier((force, *terms_z))
    terms_z = exchange(terms_z)
    terms_x = along_x(diffusivity, fields, cell, force)
    gathered = rows & (rows - 1) == 0 and rows * fields.size * 4 <= 16 * MIB
    if gathered:
        own = (fields, *along_y(place, near, fields, payload, others, (terms_x, terms_z)))
    else:
        terms_x = terms_x + pencil_along_y(diffusivity, fields)
        pairs = [(i, i + 1) for i in range(1, rows - 1, 2)]
        far = payload[fields.size // fields.shape[3]:]
        own = (
            lax.ppermute(near, "row", [(i, i ^ 1) for i in range(rows) if i ^ 1 < rows]),
            lax.ppermute(far, "row", pairs + [(b, a) for a, b in pairs]),
        )
    tendency, arrivals = total(gathered, place, diffusivity, terms_x, own, terms_z)
    return (tendency, kept, arrivals.transpose(1, 0, 2))


def solution(mesh):
    return jax.shard_map(
        on_device,
        mesh=mesh,
        in_specs=(
            P(None, "row", None, "col"),
            P(),
            P(None, ("row", "col")),
            P(("row", "col")),
            P(("row", "col")),
            P(("row", "col")),
            P(("row", "col")),
            P(("row", "col")),
        ),
        out_specs=(
            P(None, "row", None, "col"),
            P(None, ("row", "col")),
            P(None, None, ("row", "col")),
        ),
        check_vma=False,
    )
```

```python
import functools

import jax
import jax.numpy as jnp
import ml_dtypes
import numpy as np
from jax import lax
from jax.experimental import pallas as pl
from jax.experimental.pallas import tpu as pltpu
from jax.sharding import PartitionSpec as P

MIG = 256
LANES = 128
MIB = 1 << 20

time_step = 0.2
coupling = 0.5
stretch = 1.5


def periodic_compact(points):
    index = np.arange(points)
    offset = (index[None, :] - index[:, None]) % points
    lhs = (offset == 0) + ((offset == 1) | (offset == points - 1)) / 3.0
    rhs = 7.0 / 9.0 * ((offset == 1) * 1.0 - (offset == points - 1))
    rhs = rhs + ((offset == 2) * 1.0 - (offset == points - 2)) / 36.0
    return np.linalg.solve(lhs, rhs)


def wall_compact(points):
    lhs = np.eye(points)
    rhs = np.zeros((points, points))
    for row in range(points):
        if row == 0:
            lhs[0, 1] = 2.0
            rhs[0, :3] = (-2.5, 2.0, 0.5)
        elif row == points - 1:
            lhs[row, row - 1] = 2.0
            rhs[row, -3:] = (-0.5, -2.0, 2.5)
        elif row in (1, points - 2):
            lhs[row, [row - 1, row + 1]] = 0.25
            rhs[row, [row - 1, row + 1]] = (-0.75, 0.75)
        else:
            lhs[row, [row - 1, row + 1]] = 1.0 / 3.0
            rhs[row, [row - 2, row - 1, row + 1, row + 2]] = (-1 / 36, -7 / 9, 7 / 9, 1 / 36)
    coord = -1.0 + 2.0 * np.arange(points) / (points - 1)
    slope = stretch * (1.0 - np.tanh(stretch * coord) ** 2) / np.tanh(stretch)
    return np.linalg.solve(lhs, rhs) / slope[:, None]


def spectral_matrix(points):
    index = np.arange(points)
    offset = index[:, None] - index[None, :]
    parity = 1 - 2 * (offset % 2)
    angle = np.pi * np.where(offset == 0, 1, offset) / points
    return np.where(offset == 0, 0.0, np.pi / points * parity / np.tan(angle))


def two_terms(matrix):
    exact = np.asarray(matrix, np.float32)
    high = exact.astype(ml_dtypes.bfloat16)
    low = (exact - high.astype(np.float32)).astype(ml_dtypes.bfloat16)
    return high, low


def split(value, terms):
    pieces = []
    for _ in range(terms):
        piece = value.astype(jnp.bfloat16)
        pieces.append(piece)
        value = value - piece.astype(jnp.float32)
    return pieces


def dot(a, b):
    return lax.dot_general(a, b, (((1,), (0,)), ((), ())), preferred_element_type=jnp.float32)


def dot_transposed(a, b):
    return lax.dot_general(a, b, (((1,), (1,)), ((), ())), preferred_element_type=jnp.float32)


def sublane_iota(rows, columns, dtype=jnp.int32):
    return lax.broadcasted_iota(dtype, (rows, columns), 0)


def is_row(rows, index):
    return sublane_iota(rows, index.shape[1], jnp.int16) == index.astype(jnp.int16)


def one_hot(rows, index):
    return jnp.where(is_row(rows, index), jnp.bfloat16(1), jnp.bfloat16(0))


def divide(value, by):
    if by & (by - 1):
        return lax.div(value, by), lax.rem(value, by)
    return lax.shift_right_logical(value, by.bit_length() - 1), value & (by - 1)


def chunk_of(particles, rows):
    chunk = particles
    while chunk * rows > 1 << 20 and chunk % 256 == 0:
        chunk //= 2
    return chunk


def params(mib):
    return pltpu.CompilerParams(vmem_limit_bytes=mib * MIB)


CHEAP = pl.CostEstimate(flops=1, bytes_accessed=1, transcendentals=0)
LONG = pl.CostEstimate(flops=20 * 10**9, bytes_accessed=100 * 10**6, transcendentals=0)


def any_space(shape):
    return jax.ShapeDtypeStruct(tuple(shape), jnp.float32)


VMEM = pl.BlockSpec(memory_space=pltpu.VMEM)
SMEM = pl.BlockSpec(memory_space=pltpu.SMEM)


def advance_kernel(chunk, row_ref, count_ref, fields_ref, records_ref, response_ref, cell_ref, destination_ref,
                   slot_ref, kept_ref, force_ref, near_ref, far_ref, side_ref, table_ref, total_ref):
    planes, width, lanes = fields_ref.shape[1:]
    rows = planes * width
    particles = records_ref.shape[1]
    for component in range(3):
        plane = fields_ref[component].reshape(rows, lanes).T
        high, low = split(plane, 2)
        table_ref[component * lanes:(component + 1) * lanes, :rows] = high
        table_ref[component * lanes:(component + 1) * lanes, rows:] = low
    groups = 4 * MIG // LANES

    def step(index, sums):
        window = pl.ds(index * chunk, chunk)
        cell = cell_ref[:, window]
        row, lane = divide(cell, lanes)
        row_hot = one_hot(rows, row)
        found = dot(table_ref[...], jnp.concatenate([row_hot, row_hot], axis=0))
        at_lane = sublane_iota(lanes, chunk) == lane
        fluid = jnp.concatenate(
            [jnp.sum(jnp.where(at_lane, found[a * lanes:(a + 1) * lanes], 0.0), axis=0, keepdims=True) for a in range(3)],
            axis=0)
        records = records_ref[:, window]
        speed = records[3:6]
        drag = (fluid - speed) / response_ref[:, window]
        velocity = speed + time_step * drag
        moved = jnp.concatenate([records[0:3] + time_step * velocity, velocity], axis=0)
        live = index * chunk + lax.broadcasted_iota(jnp.int32, (1, chunk), 1) < count_ref[...]
        destination = destination_ref[:, window]
        kept_ref[:, window] = jnp.where(live & (destination == 0), moved, 0.0)
        force_ref[:, window] = jnp.where(live, -coupling * drag, 0.0)
        leaving = live & (destination > 0)
        group, place = divide(slot_ref[:, window], LANES)
        group = jnp.where(leaving, (destination - 1) * (MIG // LANES) + group, -1)
        slot_hot = one_hot(LANES, place)
        padded = jnp.concatenate([moved, jnp.zeros((2, chunk), jnp.float32)], axis=0)
        pieces = []
        for _ in range(2):
            piece = padded.astype(jnp.bfloat16).astype(jnp.float32)
            padded = padded - piece
            pieces += [jnp.where(group == g, piece, 0.0) for g in range(groups)]
        sent = jnp.concatenate(pieces, axis=0).astype(jnp.bfloat16)
        return sums + dot_transposed(sent, slot_hot)

    total_ref[...] = jnp.zeros_like(total_ref)
    if chunk == particles:
        total_ref[...] = step(0, total_ref[...])
    else:
        def loop(index, carry):
            total_ref[...] = step(pl.multiple_of(index, 1), total_ref[...])
            return carry

        lax.fori_loop(0, particles // chunk, loop, 0)
    outgoing = (total_ref[:8 * groups] + total_ref[8 * groups:]).reshape(4, groups // 4, 8, LANES)
    even = lax.rem(row_ref[0], 2) == 0
    near_ref[...] = jnp.where(even, outgoing[0], outgoing[1])
    side_ref[...] = outgoing[2:]
    far_ref[...] = jnp.where(even, outgoing[1], outgoing[0])


def advance(row, counts, fields, records, response, cell, destination, slot):
    planes, width, lanes = fields.shape[1:]
    rows = planes * width
    particles = records.shape[1]
    groups = 4 * MIG // LANES
    box = (groups // 4, 8, LANES)
    return pl.pallas_call(
        functools.partial(advance_kernel, chunk_of(particles, rows)),
        out_shape=(any_space((6, particles)), any_space((3, particles)), any_space(box), any_space(box), any_space((2, *box))),
        in_specs=[SMEM] + [VMEM] * 7,
        out_specs=(VMEM,) * 5,
        scratch_shapes=[pltpu.VMEM((3 * lanes, 2 * rows), jnp.bfloat16), pltpu.VMEM((16 * groups, LANES), jnp.float32)],
        compiler_params=params(40),
        cost_estimate=CHEAP,
        name="advance",
    )(row, counts, fields, records, response, cell, destination, slot)


def along_xy_kernel(chunk, viscous_ref, fields_ref, operator_ref, cell_ref, force_ref, *refs):
    *y_refs, out_ref, total_ref = refs
    if y_refs:
        *y_refs, out_ref, sibling_ref, total_ref = refs
    parts, planes, width, lanes = fields_ref.shape
    rows = planes * width
    half = rows // 2
    particles = cell_ref.shape[1]
    total_ref[...] = jnp.zeros_like(total_ref)

    def step(index):
        window = pl.ds(index * chunk, chunk)
        cell = cell_ref[:, window]
        row, lane = divide(cell, lanes)
        part, row = divide(row, half)
        column = part * lanes + lane
        at_row = is_row(half, row)
        column_hot = one_hot(2 * lanes, column)
        pieces = []
        force = force_ref[:, window]
        for _ in range(2):
            piece = force.astype(jnp.bfloat16)
            force = force - piece.astype(jnp.float32)
            pieces += [jnp.where(at_row, piece[a:a + 1], jnp.bfloat16(0)) for a in range(3)]
        return dot_transposed(jnp.concatenate(pieces, axis=0), column_hot)

    if chunk == particles:
        total_ref[...] = step(0)
    else:
        def loop(index, carry):
            total_ref[...] += step(index)
            return carry

        lax.fori_loop(0, particles // chunk, loop, 0)
    for component in range(parts):
        viscous = viscous_ref[component]
        for plane in range(planes):
            field = fields_ref[component, plane]
            high, low = split(field, 2)
            stacked = jnp.concatenate([high, low, high], axis=0)
            both = dot(operator_ref[...], stacked)
            value = -fields_ref[0, plane] * both[:width] + viscous * both[width:]
            if component < 3:
                for start in range(plane * width, (plane + 1) * width, min(width, half)):
                    part, first = divmod(start, half)
                    size = min(width, half)
                    columns = slice(part * lanes, (part + 1) * lanes)
                    base = component * half + first
                    deposit = (total_ref[base:base + size, columns]
                               + total_ref[3 * half + base:3 * half + base + size, columns])
                    inside = start - plane * width
                    out_ref[component, plane, inside:inside + size] = value[inside:inside + size] + deposit
            else:
                out_ref[component, plane] = value
    if not y_refs:
        return
    row_ref, weight_ref, near_ref, mate_ref, *others = y_refs
    count = 2 * (len(others) + 1)
    size = parts * planes * width
    mine = row_ref[0] * (count * planes * planes * 2)
    step = min(width, 32)
    for component in range(parts):
        for first in range(0, width, step):
            inside = slice(first, first + step)
            sums = [[None] * 2 for _ in range(2 * planes)]
            for index in range(count // 2):
                block = others[index - 1] if index else fields_ref
                for source in range(planes):
                    value = block[component, source, inside]
                    for target in range(2 * planes):
                        for kind in range(2):
                            weight = weight_ref[mine + ((index * planes + source) * 2 * planes + target) * 2 + kind]
                            before = sums[target][kind]
                            sums[target][kind] = weight * value if before is None else before + weight * value
            for plane in range(planes):
                along, curve = sums[plane]
                out_ref[component, plane, inside] += viscous_ref[component] * curve - fields_ref[1, plane, inside] * along
                along, curve = sums[planes + plane]
                row = (component * planes + plane) * width + first
                sibling_ref[row:row + step] = viscous_ref[component] * curve - mate_ref[1, plane, inside] * along
    sibling_ref[size:] = near_ref[...].reshape(MIG // LANES * 8, lanes)


def same_core(block, s):
    return lax.ppermute(block, "row", [(i, i ^ s) for i in range(lax.axis_size("row"))])


def along_y_weights(rows, planes):
    deriv = wall_compact(rows * planes)
    operators = np.stack([deriv, deriv @ deriv], axis=-1)
    table = np.zeros((rows, rows // 2, planes, 2, planes, 2), np.float32)
    for me in range(rows):
        for index in range(rows // 2):
            for side in range(2):
                target, source = (me ^ side) * planes, (me ^ (2 * index)) * planes
                block = operators[target:target + planes, source:source + planes]
                table[me, index, :, side] = block.transpose(1, 0, 2)
    return jnp.asarray(table.reshape(-1))


def along_xy(viscous, fields, cell, force, y_part):
    parts, planes, width, lanes = fields.shape
    half = planes * width // 2
    particles = cell.shape[1]
    deriv = periodic_compact(width)
    high, low = two_terms(np.concatenate([deriv, deriv @ deriv], axis=0))
    operator = jnp.asarray(np.concatenate([high, high, low], axis=1))
    specs, outs = [], [any_space(fields.shape)]
    if y_part:
        row, near, mate, others = y_part
        y_part = (row, along_y_weights(lax.axis_size("row"), planes), near, mate, *others)
        specs = [SMEM] * 2 + [VMEM] * (2 + len(others))
        outs.append(any_space((fields.size // lanes + MIG // LANES * 8, lanes)))
    return pl.pallas_call(
        functools.partial(along_xy_kernel, chunk_of(particles, 2 * half)),
        out_shape=tuple(outs),
        in_specs=[SMEM] + [VMEM] * 4 + specs,
        out_specs=(VMEM,) * len(outs),
        scratch_shapes=[pltpu.VMEM((6 * half, 2 * lanes), jnp.float32)],
        compiler_params=params(40),
        cost_estimate=CHEAP,
        name="along_xy",
    )(viscous, fields, operator, cell, force, *y_part)


def along_z_kernel(viscous_ref, high_ref, low_ref, side_ref, *refs):
    count = len(refs) // 2
    blocks, results = refs[:count], refs[count:]
    parts, planes, width, lanes = blocks[0].shape
    rows = parts * planes * width
    pieces = [split(block[...].reshape(rows, lanes), 2) for block in blocks]

    def lines(term):
        return jnp.concatenate(
            [jnp.concatenate([pieces[(d - s) % count][term] for d in range(count)], axis=1) for s in range(count)], axis=0)

    high = lines(0)
    both = dot(high, high_ref[...]) + dot(lines(1), high_ref[...]) + dot(high, low_ref[...])
    for s in range(count):
        speed = blocks[(-s) % count][2]
        for component in range(parts):
            first = s * rows + component * planes * width
            part = both[first:first + planes * width]
            along = part[:, :lanes].reshape(planes, width, lanes)
            curve = part[:, lanes:].reshape(planes, width, lanes)
            value = -speed * along + viscous_ref[component] * curve
            results[s][component * planes * width:(component + 1) * planes * width] = value.reshape(planes * width, lanes)
        row = rows
        for direction in riding(s, count):
            for group in range(side_ref.shape[1]):
                results[s][row:row + 8] = side_ref[direction - 2, group]
                row += 8


def riding(s, count):
    return [direction for direction, step in ((2, 1), (3, -1)) if s == step % count]


def along_z(viscous, side, blocks):
    count = len(blocks)
    shape = blocks[0].shape
    lanes = shape[3]
    points = count * lanes
    deriv = spectral_matrix(points)
    second = deriv @ deriv
    weights = [
        np.concatenate([matrix[d * lanes:(d + 1) * lanes, :lanes].T for matrix in (deriv, second)], axis=1)
        for d in range(count)
    ]
    high, low = two_terms(np.concatenate(weights, axis=0))
    size = int(np.prod(shape))
    return pl.pallas_call(
        along_z_kernel,
        out_shape=tuple(any_space((size // lanes + MIG // LANES * 8 * len(riding(s, count)), lanes)) for s in range(count)),
        in_specs=[SMEM] + [VMEM] * (3 + count),
        out_specs=(VMEM,) * count,
        compiler_params=params(48),
        cost_estimate=CHEAP,
        name="along_z",
    )(viscous, jnp.asarray(high), jnp.asarray(low), side, *blocks)


def pencil_along_y(viscous, fields):
    highest = lax.Precision.HIGHEST
    pencil = lax.all_to_all(fields, "row", split_axis=2, concat_axis=1, tiled=True)
    deriv = wall_compact(pencil.shape[1])
    operators = [jnp.asarray(matrix, jnp.float32) for matrix in (deriv, deriv @ deriv)]
    along, curve = (jnp.einsum("ij,cjxz->cixz", matrix, pencil, precision=highest) for matrix in operators)
    partial = -pencil[1] * along + viscous[:, None, None, None] * curve
    return lax.all_to_all(partial, "row", split_axis=1, concat_axis=2, tiled=True)


def side_kernel(first, *refs):
    blocks, out_ref = refs[:-1], refs[-1]
    for s, block in enumerate(blocks):
        row = first
        for direction in riding(s, len(blocks)):
            for group in range(out_ref.shape[1]):
                out_ref[direction - 2, group] = block[row:row + 8]
                row += 8


def side_particles(blocks):
    first = min(block.shape[0] for block in blocks)
    return pl.pallas_call(
        functools.partial(side_kernel, first),
        out_shape=any_space((2, MIG // LANES, 8, LANES)),
        in_specs=[VMEM] * len(blocks),
        out_specs=VMEM,
        compiler_params=params(8),
        cost_estimate=LONG,
        name="side_particles",
    )(*blocks)


def total_kernel(gathered, row_ref, column_ref, along_x_ref, far_ref, side_ref, near_ref, *refs):
    blocks, out_ref, arrivals_ref = refs[:-2], refs[-2], refs[-1]
    count = len(blocks)
    parts, planes, width, lanes = out_ref.shape
    size = width // count
    whole = parts * planes * width
    for s, block in enumerate(blocks):
        start = pl.multiple_of(lax.rem(column_ref[0] + count - s, count) * size, size)
        rows = pl.ds(start, size)
        for component in range(parts):
            for plane in range(planes):
                first = (component * planes + plane) * size
                value = along_x_ref[component, plane, rows, :] + block[first:first + size]
                if gathered:
                    row = pl.multiple_of((component * planes + plane) * width + start, size)
                    value += near_ref[pl.ds(row, size)]
                out_ref[component, plane, rows, :] = value
    even = lax.rem(row_ref[0], 2) == 0
    for group in range(MIG // LANES):
        columns = slice(group * LANES, (group + 1) * LANES)
        if gathered:
            near = near_ref[whole + group * 8:whole + group * 8 + 6]
        else:
            near = near_ref[group, :6]
        far = far_ref[group, :6]
        arrivals_ref[:, 0, columns] = jnp.where(even, far, near)
        arrivals_ref[:, 1, columns] = jnp.where(even, near, far)
        for direction in (2, 3):
            arrivals_ref[:, direction, columns] = side_ref[direction - 2, group, :6]


def total(gathered, row, column, along_x_part, far, side, near, blocks):
    size = along_x_part.size
    return pl.pallas_call(
        functools.partial(total_kernel, gathered),
        out_shape=(any_space(along_x_part.shape), any_space((6, 4, MIG))),
        in_specs=[SMEM] * 2 + [VMEM] * (4 + len(blocks)),
        out_specs=(VMEM, VMEM),
        compiler_params=params(32),
        cost_estimate=CHEAP,
        name="total",
    )(row, column, along_x_part, far, side, near, *blocks)


def exchange(blocks):
    count = lax.axis_size("col")
    received = list(blocks)
    for s in sorted(range(1, count), key=lambda s: -min(s, count - s)):
        received[s] = lax.ppermute(blocks[s], "col", [(i, (i + s) % count) for i in range(count)])
    return received


def on_device(fields, diffusivity, records, response_time, cell_index, counts, destination, slot):
    rows, columns = lax.axis_size("row"), lax.axis_size("col")
    row, column = lax.axis_index("row"), lax.axis_index("col")
    width = fields.shape[2] // columns
    cell = cell_index.reshape(1, -1)
    blocks = [
        lax.dynamic_slice_in_dim(fields, (column + s) % columns * width, width, axis=2) for s in range(columns)
    ]
    row, column = row.reshape(1), column.reshape(1)
    gathered = rows & (rows - 1) == 0 and rows * fields.size * 4 <= 16 * MIB
    if gathered:
        mate = same_core(fields, 1)
        mate, blocks = lax.optimization_barrier((mate, blocks))
    lines = exchange(blocks)
    others = [same_core(fields, s) for s in range(2, rows - 2, 2)] if gathered else []
    kept, force, near, far, side = advance(
        row, counts.reshape(1, 1), fields, records, response_time.reshape(1, -1), cell, destination.reshape(1, -1),
        slot.reshape(1, -1))
    side, lines, others, later = lax.optimization_barrier((side, lines, others, fields))
    pairs = [(i, i + 1) for i in range(1, rows - 1, 2)]
    far = lax.ppermute(far, "row", pairs + [(b, a) for a, b in pairs])
    if gathered:
        others.append(same_core(later, rows - 2))
    terms_z = exchange(along_z(diffusivity, side, lines))
    terms_x, *near_y = along_xy(diffusivity, fields, cell, force, (row, near, mate, others) if gathered else ())
    if gathered:
        near = same_core(near_y[0], 1)
    else:
        terms_x = terms_x + pencil_along_y(diffusivity, fields)
        near = lax.ppermute(near, "row", [(i, i ^ 1) for i in range(rows) if i ^ 1 < rows])
    tendency, arrivals = total(gathered, row, column, terms_x, far, side_particles(terms_z), near, terms_z)
    return (tendency, kept, arrivals.transpose(1, 0, 2))


def solution(mesh):
    return jax.shard_map(
        on_device,
        mesh=mesh,
        in_specs=(
            P(None, "row", None, "col"),
            P(),
            P(None, ("row", "col")),
            P(("row", "col")),
            P(("row", "col")),
            P(("row", "col")),
            P(("row", "col")),
            P(("row", "col")),
        ),
        out_specs=(
            P(None, "row", None, "col"),
            P(None, ("row", "col")),
            P(None, None, ("row", "col")),
        ),
        check_vma=False,
    )
```

```python
import functools

import jax
import jax.numpy as jnp
import ml_dtypes
import numpy as np
from jax import lax
from jax.experimental import pallas as pl
from jax.experimental.pallas import tpu as pltpu
from jax.sharding import PartitionSpec as P

MIG = 256
LANES = 128
MIB = 1 << 20

time_step = 0.2
coupling = 0.5
stretch = 1.5


def periodic_compact(points):
    index = np.arange(points)
    offset = (index[None, :] - index[:, None]) % points
    lhs = (offset == 0) + ((offset == 1) | (offset == points - 1)) / 3.0
    rhs = 7.0 / 9.0 * ((offset == 1) * 1.0 - (offset == points - 1))
    rhs = rhs + ((offset == 2) * 1.0 - (offset == points - 2)) / 36.0
    return np.linalg.solve(lhs, rhs)


def wall_compact(points):
    lhs = np.eye(points)
    rhs = np.zeros((points, points))
    for row in range(points):
        if row == 0:
            lhs[0, 1] = 2.0
            rhs[0, :3] = (-2.5, 2.0, 0.5)
        elif row == points - 1:
            lhs[row, row - 1] = 2.0
            rhs[row, -3:] = (-0.5, -2.0, 2.5)
        elif row in (1, points - 2):
            lhs[row, [row - 1, row + 1]] = 0.25
            rhs[row, [row - 1, row + 1]] = (-0.75, 0.75)
        else:
            lhs[row, [row - 1, row + 1]] = 1.0 / 3.0
            rhs[row, [row - 2, row - 1, row + 1, row + 2]] = (-1 / 36, -7 / 9, 7 / 9, 1 / 36)
    coord = -1.0 + 2.0 * np.arange(points) / (points - 1)
    slope = stretch * (1.0 - np.tanh(stretch * coord) ** 2) / np.tanh(stretch)
    return np.linalg.solve(lhs, rhs) / slope[:, None]


def spectral_matrix(points):
    index = np.arange(points)
    offset = index[:, None] - index[None, :]
    parity = 1 - 2 * (offset % 2)
    angle = np.pi * np.where(offset == 0, 1, offset) / points
    return np.where(offset == 0, 0.0, np.pi / points * parity / np.tan(angle))


def two_terms(matrix):
    exact = np.asarray(matrix, np.float32)
    high = exact.astype(ml_dtypes.bfloat16)
    low = (exact - high.astype(np.float32)).astype(ml_dtypes.bfloat16)
    return high, low


def split(value, terms):
    pieces = []
    for _ in range(terms):
        piece = value.astype(jnp.bfloat16)
        pieces.append(piece)
        value = value - piece.astype(jnp.float32)
    return pieces


def dot(a, b):
    return lax.dot_general(a, b, (((1,), (0,)), ((), ())), preferred_element_type=jnp.float32)


def dot_transposed(a, b):
    return lax.dot_general(a, b, (((1,), (1,)), ((), ())), preferred_element_type=jnp.float32)


def sublane_iota(rows, columns, dtype=jnp.int32):
    return lax.broadcasted_iota(dtype, (rows, columns), 0)


def is_row(rows, index):
    return sublane_iota(rows, index.shape[1], jnp.int16) == index.astype(jnp.int16)


def one_hot(rows, index):
    return jnp.where(is_row(rows, index), jnp.bfloat16(1), jnp.bfloat16(0))


def divide(value, by):
    if by & (by - 1):
        return lax.div(value, by), lax.rem(value, by)
    return lax.shift_right_logical(value, by.bit_length() - 1), value & (by - 1)


def chunk_of(particles, rows):
    chunk = particles
    while chunk * rows > 1 << 20 and chunk % 256 == 0:
        chunk //= 2
    return chunk


def params(mib):
    return pltpu.CompilerParams(vmem_limit_bytes=mib * MIB)


CHEAP = pl.CostEstimate(flops=1, bytes_accessed=1, transcendentals=0)
LONG = pl.CostEstimate(flops=20 * 10**9, bytes_accessed=100 * 10**6, transcendentals=0)


def any_space(shape):
    return jax.ShapeDtypeStruct(tuple(shape), jnp.float32)


VMEM = pl.BlockSpec(memory_space=pltpu.VMEM)
SMEM = pl.BlockSpec(memory_space=pltpu.SMEM)


def advance_kernel(chunk, row_ref, count_ref, fields_ref, records_ref, response_ref, cell_ref, destination_ref,
                   slot_ref, kept_ref, force_ref, near_ref, far_ref, side_ref, table_ref, total_ref):
    planes, width, lanes = fields_ref.shape[1:]
    rows = planes * width
    particles = records_ref.shape[1]
    for component in range(3):
        plane = fields_ref[component].reshape(rows, lanes).T
        high, low = split(plane, 2)
        table_ref[component * lanes:(component + 1) * lanes, :rows] = high
        table_ref[component * lanes:(component + 1) * lanes, rows:] = low
    groups = 4 * MIG // LANES

    def step(index, sums):
        window = pl.ds(index * chunk, chunk)
        cell = cell_ref[:, window]
        row, lane = divide(cell, lanes)
        row_hot = one_hot(rows, row)
        found = dot(table_ref[...], jnp.concatenate([row_hot, row_hot], axis=0))
        at_lane = sublane_iota(lanes, chunk) == lane
        fluid = jnp.concatenate(
            [jnp.sum(jnp.where(at_lane, found[a * lanes:(a + 1) * lanes], 0.0), axis=0, keepdims=True) for a in range(3)],
            axis=0)
        records = records_ref[:, window]
        speed = records[3:6]
        drag = (fluid - speed) / response_ref[:, window]
        velocity = speed + time_step * drag
        moved = jnp.concatenate([records[0:3] + time_step * velocity, velocity], axis=0)
        live = index * chunk + lax.broadcasted_iota(jnp.int32, (1, chunk), 1) < count_ref[...]
        destination = destination_ref[:, window]
        kept_ref[:, window] = jnp.where(live & (destination == 0), moved, 0.0)
        force_ref[:, window] = jnp.where(live, -coupling * drag, 0.0)
        leaving = live & (destination > 0)
        group, place = divide(slot_ref[:, window], LANES)
        group = jnp.where(leaving, (destination - 1) * (MIG // LANES) + group, -1)
        slot_hot = one_hot(LANES, place)
        padded = jnp.concatenate([moved, jnp.zeros((2, chunk), jnp.float32)], axis=0)
        pieces = []
        for _ in range(2):
            piece = padded.astype(jnp.bfloat16).astype(jnp.float32)
            padded = padded - piece
            pieces += [jnp.where(group == g, piece, 0.0) for g in range(groups)]
        sent = jnp.concatenate(pieces, axis=0).astype(jnp.bfloat16)
        return sums + dot_transposed(sent, slot_hot)

    total_ref[...] = jnp.zeros_like(total_ref)
    if chunk == particles:
        total_ref[...] = step(0, total_ref[...])
    else:
        def loop(index, carry):
            total_ref[...] = step(pl.multiple_of(index, 1), total_ref[...])
            return carry

        lax.fori_loop(0, particles // chunk, loop, 0)
    outgoing = (total_ref[:8 * groups] + total_ref[8 * groups:]).reshape(4, groups // 4, 8, LANES)
    even = lax.rem(row_ref[0], 2) == 0
    near_ref[...] = jnp.where(even, outgoing[0], outgoing[1])
    side_ref[...] = outgoing[2:]
    far_ref[...] = jnp.where(even, outgoing[1], outgoing[0])


def advance(row, counts, fields, records, response, cell, destination, slot):
    planes, width, lanes = fields.shape[1:]
    rows = planes * width
    particles = records.shape[1]
    groups = 4 * MIG // LANES
    box = (groups // 4, 8, LANES)
    return pl.pallas_call(
        functools.partial(advance_kernel, chunk_of(particles, rows)),
        out_shape=(any_space((6, particles)), any_space((3, particles)), any_space(box), any_space(box), any_space((2, *box))),
        in_specs=[SMEM] + [VMEM] * 7,
        out_specs=(VMEM,) * 5,
        scratch_shapes=[pltpu.VMEM((3 * lanes, 2 * rows), jnp.bfloat16), pltpu.VMEM((16 * groups, LANES), jnp.float32)],
        compiler_params=params(40),
        cost_estimate=CHEAP,
        name="advance",
    )(row, counts, fields, records, response, cell, destination, slot)


def along_xy_kernel(chunk, viscous_ref, fields_ref, operator_ref, cell_ref, force_ref, *refs):
    *y_refs, out_ref, total_ref = refs
    if y_refs:
        *y_refs, out_ref, sibling_ref, total_ref = refs
    parts, planes, width, lanes = fields_ref.shape
    rows = planes * width
    half = rows // 2
    particles = cell_ref.shape[1]
    total_ref[...] = jnp.zeros_like(total_ref)

    def step(index):
        window = pl.ds(index * chunk, chunk)
        cell = cell_ref[:, window]
        row, lane = divide(cell, lanes)
        part, row = divide(row, half)
        column = part * lanes + lane
        at_row = is_row(half, row)
        column_hot = one_hot(2 * lanes, column)
        pieces = []
        force = force_ref[:, window]
        for _ in range(2):
            piece = force.astype(jnp.bfloat16)
            force = force - piece.astype(jnp.float32)
            pieces += [jnp.where(at_row, piece[a:a + 1], jnp.bfloat16(0)) for a in range(3)]
        return dot_transposed(jnp.concatenate(pieces, axis=0), column_hot)

    if chunk == particles:
        total_ref[...] = step(0)
    else:
        def loop(index, carry):
            total_ref[...] += step(index)
            return carry

        lax.fori_loop(0, particles // chunk, loop, 0)
    for component in range(parts):
        viscous = viscous_ref[component]
        for plane in range(planes):
            field = fields_ref[component, plane]
            high, low = split(field, 2)
            stacked = jnp.concatenate([high, low, high], axis=0)
            both = dot(operator_ref[...], stacked)
            value = -fields_ref[0, plane] * both[:width] + viscous * both[width:]
            if component < 3:
                for start in range(plane * width, (plane + 1) * width, min(width, half)):
                    part, first = divmod(start, half)
                    size = min(width, half)
                    columns = slice(part * lanes, (part + 1) * lanes)
                    base = component * half + first
                    deposit = (total_ref[base:base + size, columns]
                               + total_ref[3 * half + base:3 * half + base + size, columns])
                    inside = start - plane * width
                    out_ref[component, plane, inside:inside + size] = value[inside:inside + size] + deposit
            else:
                out_ref[component, plane] = value
    if not y_refs:
        return
    row_ref, weight_ref, near_ref, mate_ref, *others = y_refs
    both_ref, diagonal_ref = others
    blocks = [fields_ref, diagonal_ref, both_ref.at[0], both_ref.at[1]]
    size = parts * planes * width
    mine = row_ref[0] * (len(blocks) * planes * 2 * planes * 2)
    step = min(width, 32)
    for component in range(parts):
        for first in range(0, width, step):
            inside = slice(first, first + step)
            sums = [[None] * 2 for _ in range(2 * planes)]
            for index, block in enumerate(blocks):
                for source in range(planes):
                    value = block[component, source, inside]
                    for target in range(2 * planes):
                        for kind in range(2):
                            weight = weight_ref[mine + ((index * planes + source) * 2 * planes + target) * 2 + kind]
                            before = sums[target][kind]
                            sums[target][kind] = weight * value if before is None else before + weight * value
            for plane in range(planes):
                along, curve = sums[plane]
                out_ref[component, plane, inside] += viscous_ref[component] * curve - fields_ref[1, plane, inside] * along
                along, curve = sums[planes + plane]
                row = (component * planes + plane) * width + first
                sibling_ref[row:row + step] = viscous_ref[component] * curve - mate_ref[1, plane, inside] * along
    sibling_ref[size:] = near_ref[...].reshape(MIG // LANES * 8, lanes)


def same_core(block, s):
    return lax.ppermute(block, "row", [(i, i ^ s) for i in range(lax.axis_size("row"))])


def neighbour(row):
    return row ^ 4 if row % 2 else row ^ 2


def along_y_weights(rows, planes):
    deriv = wall_compact(rows * planes)
    operators = np.stack([deriv, deriv @ deriv], axis=-1)
    table = np.zeros((rows, 4, planes, 2, planes, 2), np.float32)
    for me in range(rows):
        for index, other in enumerate((me, me ^ 6, neighbour(me), neighbour(me) ^ 1)):
            for side in range(2):
                target, source = (me ^ side) * planes, other * planes
                block = operators[target:target + planes, source:source + planes]
                table[me, index, :, side] = block.transpose(1, 0, 2)
    return jnp.asarray(table.reshape(-1))


def along_xy(viscous, fields, cell, force, y_part):
    parts, planes, width, lanes = fields.shape
    half = planes * width // 2
    particles = cell.shape[1]
    deriv = periodic_compact(width)
    high, low = two_terms(np.concatenate([deriv, deriv @ deriv], axis=0))
    operator = jnp.asarray(np.concatenate([high, high, low], axis=1))
    specs, outs = [], [any_space(fields.shape)]
    if y_part:
        row, near, mate, others = y_part
        y_part = (row, along_y_weights(lax.axis_size("row"), planes), near, mate, *others)
        specs = [SMEM] * 2 + [VMEM] * (2 + len(others))
        outs.append(any_space((fields.size // lanes + MIG // LANES * 8, lanes)))
    return pl.pallas_call(
        functools.partial(along_xy_kernel, chunk_of(particles, 2 * half)),
        out_shape=tuple(outs),
        in_specs=[SMEM] + [VMEM] * 4 + specs,
        out_specs=(VMEM,) * len(outs),
        scratch_shapes=[pltpu.VMEM((6 * half, 2 * lanes), jnp.float32)],
        compiler_params=params(40),
        cost_estimate=LONG,
        name="along_xy",
    )(viscous, fields, operator, cell, force, *y_part)


def along_z_kernel(viscous_ref, high_ref, low_ref, side_ref, *refs):
    count = len(refs) // 2
    blocks, results = refs[:count], refs[count:]
    parts, planes, width, lanes = blocks[0].shape
    rows = parts * planes * width
    pieces = [split(block[...].reshape(rows, lanes), 2) for block in blocks]

    def lines(term):
        return jnp.concatenate(
            [jnp.concatenate([pieces[(d - s) % count][term] for d in range(count)], axis=1) for s in range(count)], axis=0)

    high = lines(0)
    both = dot(high, high_ref[...]) + dot(lines(1), high_ref[...]) + dot(high, low_ref[...])
    for s in range(count):
        speed = blocks[(-s) % count][2]
        for component in range(parts):
            first = s * rows + component * planes * width
            part = both[first:first + planes * width]
            along = part[:, :lanes].reshape(planes, width, lanes)
            curve = part[:, lanes:].reshape(planes, width, lanes)
            value = -speed * along + viscous_ref[component] * curve
            results[s][component * planes * width:(component + 1) * planes * width] = value.reshape(planes * width, lanes)
        row = rows
        for direction in riding(s, count):
            for group in range(side_ref.shape[1]):
                results[s][row:row + 8] = side_ref[direction - 2, group]
                row += 8


def riding(s, count):
    return [direction for direction, step in ((2, 1), (3, -1)) if s == step % count]


def along_z(viscous, side, blocks):
    count = len(blocks)
    shape = blocks[0].shape
    lanes = shape[3]
    points = count * lanes
    deriv = spectral_matrix(points)
    second = deriv @ deriv
    weights = [
        np.concatenate([matrix[d * lanes:(d + 1) * lanes, :lanes].T for matrix in (deriv, second)], axis=1)
        for d in range(count)
    ]
    high, low = two_terms(np.concatenate(weights, axis=0))
    size = int(np.prod(shape))
    return pl.pallas_call(
        along_z_kernel,
        out_shape=tuple(any_space((size // lanes + MIG // LANES * 8 * len(riding(s, count)), lanes)) for s in range(count)),
        in_specs=[SMEM] + [VMEM] * (3 + count),
        out_specs=(VMEM,) * count,
        compiler_params=params(48),
        cost_estimate=CHEAP,
        name="along_z",
    )(viscous, jnp.asarray(high), jnp.asarray(low), side, *blocks)


def pencil_along_y(viscous, fields):
    highest = lax.Precision.HIGHEST
    pencil = lax.all_to_all(fields, "row", split_axis=2, concat_axis=1, tiled=True)
    deriv = wall_compact(pencil.shape[1])
    operators = [jnp.asarray(matrix, jnp.float32) for matrix in (deriv, deriv @ deriv)]
    along, curve = (jnp.einsum("ij,cjxz->cixz", matrix, pencil, precision=highest) for matrix in operators)
    partial = -pencil[1] * along + viscous[:, None, None, None] * curve
    return lax.all_to_all(partial, "row", split_axis=1, concat_axis=2, tiled=True)


def side_kernel(first, *refs):
    blocks, out_ref = refs[:-1], refs[-1]
    for s, block in enumerate(blocks):
        row = first
        for direction in riding(s, len(blocks)):
            for group in range(out_ref.shape[1]):
                out_ref[direction - 2, group] = block[row:row + 8]
                row += 8


def side_particles(blocks):
    first = min(block.shape[0] for block in blocks)
    return pl.pallas_call(
        functools.partial(side_kernel, first),
        out_shape=any_space((2, MIG // LANES, 8, LANES)),
        in_specs=[VMEM] * len(blocks),
        out_specs=VMEM,
        compiler_params=params(8),
        cost_estimate=LONG,
        name="side_particles",
    )(*blocks)


def total_kernel(gathered, row_ref, column_ref, along_x_ref, far_ref, side_ref, near_ref, *refs):
    blocks, out_ref, arrivals_ref = refs[:-2], refs[-2], refs[-1]
    count = len(blocks)
    parts, planes, width, lanes = out_ref.shape
    size = width // count
    whole = parts * planes * width
    for s, block in enumerate(blocks):
        start = pl.multiple_of(lax.rem(column_ref[0] + count - s, count) * size, size)
        rows = pl.ds(start, size)
        for component in range(parts):
            for plane in range(planes):
                first = (component * planes + plane) * size
                value = along_x_ref[component, plane, rows, :] + block[first:first + size]
                if gathered:
                    row = pl.multiple_of((component * planes + plane) * width + start, size)
                    value += near_ref[pl.ds(row, size)]
                out_ref[component, plane, rows, :] = value
    even = lax.rem(row_ref[0], 2) == 0
    for group in range(MIG // LANES):
        columns = slice(group * LANES, (group + 1) * LANES)
        if gathered:
            near = near_ref[whole + group * 8:whole + group * 8 + 6]
        else:
            near = near_ref[group, :6]
        far = far_ref[group, :6]
        arrivals_ref[:, 0, columns] = jnp.where(even, far, near)
        arrivals_ref[:, 1, columns] = jnp.where(even, near, far)
        for direction in (2, 3):
            arrivals_ref[:, direction, columns] = side_ref[direction - 2, group, :6]


def total(gathered, row, column, along_x_part, far, side, near, blocks):
    size = along_x_part.size
    return pl.pallas_call(
        functools.partial(total_kernel, gathered),
        out_shape=(any_space(along_x_part.shape), any_space((6, 4, MIG))),
        in_specs=[SMEM] * 2 + [VMEM] * (4 + len(blocks)),
        out_specs=(VMEM, VMEM),
        compiler_params=params(32),
        cost_estimate=CHEAP,
        name="total",
    )(row, column, along_x_part, far, side, near, *blocks)


def exchange(blocks):
    count = lax.axis_size("col")
    received = list(blocks)
    for s in sorted(range(1, count), key=lambda s: -min(s, count - s)):
        received[s] = lax.ppermute(blocks[s], "col", [(i, (i + s) % count) for i in range(count)])
    return received


def on_device(fields, diffusivity, records, response_time, cell_index, counts, destination, slot):
    rows, columns = lax.axis_size("row"), lax.axis_size("col")
    row, column = lax.axis_index("row"), lax.axis_index("col")
    width = fields.shape[2] // columns
    cell = cell_index.reshape(1, -1)
    blocks = [
        lax.dynamic_slice_in_dim(fields, (column + s) % columns * width, width, axis=2) for s in range(columns)
    ]
    row, column = row.reshape(1), column.reshape(1)
    gathered = rows == 8 and rows * fields.size * 4 <= 16 * MIB
    if gathered:
        mate = same_core(fields, 1)
        mate, blocks = lax.optimization_barrier((mate, blocks))
    lines = exchange(blocks)
    others = []
    if gathered:
        both = jnp.stack([fields, mate])
        later, both = lax.optimization_barrier((fields, both))
        both = lax.ppermute(both, "row", [(i, neighbour(i)) for i in range(rows)])
        others = [both, same_core(later, 6)]
    kept, force, near, far, side = advance(
        row, counts.reshape(1, 1), fields, records, response_time.reshape(1, -1), cell, destination.reshape(1, -1),
        slot.reshape(1, -1))
    side, lines = lax.optimization_barrier((side, lines))
    pairs = [(i, i + 1) for i in range(1, rows - 1, 2)]
    far = lax.ppermute(far, "row", pairs + [(b, a) for a, b in pairs])
    terms_z = exchange(along_z(diffusivity, side, lines))
    terms_x, *near_y = along_xy(diffusivity, fields, cell, force, (row, near, mate, others) if gathered else ())
    if gathered:
        near = same_core(near_y[0], 1)
    else:
        terms_x = terms_x + pencil_along_y(diffusivity, fields)
        near = lax.ppermute(near, "row", [(i, i ^ 1) for i in range(rows) if i ^ 1 < rows])
    tendency, arrivals = total(gathered, row, column, terms_x, far, side_particles(terms_z), near, terms_z)
    return (tendency, kept, arrivals.transpose(1, 0, 2))


def solution(mesh):
    return jax.shard_map(
        on_device,
        mesh=mesh,
        in_specs=(
            P(None, "row", None, "col"),
            P(),
            P(None, ("row", "col")),
            P(("row", "col")),
            P(("row", "col")),
            P(("row", "col")),
            P(("row", "col")),
            P(("row", "col")),
        ),
        out_specs=(
            P(None, "row", None, "col"),
            P(None, ("row", "col")),
            P(None, None, ("row", "col")),
        ),
        check_vma=False,
    )
```

```python
import functools

import jax
import jax.numpy as jnp
import ml_dtypes
import numpy as np
from jax import lax
from jax.experimental import pallas as pl
from jax.experimental.pallas import tpu as pltpu
from jax.sharding import PartitionSpec as P

MIG = 256
LANES = 128
MIB = 1 << 20

time_step = 0.2
coupling = 0.5
stretch = 1.5


def periodic_compact(points):
    index = np.arange(points)
    offset = (index[None, :] - index[:, None]) % points
    lhs = (offset == 0) + ((offset == 1) | (offset == points - 1)) / 3.0
    rhs = 7.0 / 9.0 * ((offset == 1) * 1.0 - (offset == points - 1))
    rhs = rhs + ((offset == 2) * 1.0 - (offset == points - 2)) / 36.0
    return np.linalg.solve(lhs, rhs)


def wall_compact(points):
    lhs = np.eye(points)
    rhs = np.zeros((points, points))
    for row in range(points):
        if row == 0:
            lhs[0, 1] = 2.0
            rhs[0, :3] = (-2.5, 2.0, 0.5)
        elif row == points - 1:
            lhs[row, row - 1] = 2.0
            rhs[row, -3:] = (-0.5, -2.0, 2.5)
        elif row in (1, points - 2):
            lhs[row, [row - 1, row + 1]] = 0.25
            rhs[row, [row - 1, row + 1]] = (-0.75, 0.75)
        else:
            lhs[row, [row - 1, row + 1]] = 1.0 / 3.0
            rhs[row, [row - 2, row - 1, row + 1, row + 2]] = (-1 / 36, -7 / 9, 7 / 9, 1 / 36)
    coord = -1.0 + 2.0 * np.arange(points) / (points - 1)
    slope = stretch * (1.0 - np.tanh(stretch * coord) ** 2) / np.tanh(stretch)
    return np.linalg.solve(lhs, rhs) / slope[:, None]


def spectral_matrix(points):
    index = np.arange(points)
    offset = index[:, None] - index[None, :]
    parity = 1 - 2 * (offset % 2)
    angle = np.pi * np.where(offset == 0, 1, offset) / points
    return np.where(offset == 0, 0.0, np.pi / points * parity / np.tan(angle))


def two_terms(matrix):
    exact = np.asarray(matrix, np.float32)
    high = exact.astype(ml_dtypes.bfloat16)
    low = (exact - high.astype(np.float32)).astype(ml_dtypes.bfloat16)
    return high, low


def split(value, terms):
    pieces = []
    for _ in range(terms):
        piece = value.astype(jnp.bfloat16)
        pieces.append(piece)
        value = value - piece.astype(jnp.float32)
    return pieces


def dot(a, b):
    return lax.dot_general(a, b, (((1,), (0,)), ((), ())), preferred_element_type=jnp.float32)


def dot_transposed(a, b):
    return lax.dot_general(a, b, (((1,), (1,)), ((), ())), preferred_element_type=jnp.float32)


def sublane_iota(rows, columns, dtype=jnp.int32):
    return lax.broadcasted_iota(dtype, (rows, columns), 0)


def is_row(rows, index):
    return sublane_iota(rows, index.shape[1], jnp.int16) == index.astype(jnp.int16)


def one_hot(rows, index):
    return jnp.where(is_row(rows, index), jnp.bfloat16(1), jnp.bfloat16(0))


def divide(value, by):
    if by & (by - 1):
        return lax.div(value, by), lax.rem(value, by)
    return lax.shift_right_logical(value, by.bit_length() - 1), value & (by - 1)


def chunk_of(particles, rows):
    chunk = particles
    while chunk * rows > 1 << 20 and chunk % 256 == 0:
        chunk //= 2
    return chunk


def params(mib):
    return pltpu.CompilerParams(vmem_limit_bytes=mib * MIB)


CHEAP = pl.CostEstimate(flops=1, bytes_accessed=1, transcendentals=0)
LONG = pl.CostEstimate(flops=20 * 10**9, bytes_accessed=100 * 10**6, transcendentals=0)


def any_space(shape):
    return jax.ShapeDtypeStruct(tuple(shape), jnp.float32)


VMEM = pl.BlockSpec(memory_space=pltpu.VMEM)
SMEM = pl.BlockSpec(memory_space=pltpu.SMEM)


def advance_kernel(chunk, row_ref, count_ref, fields_ref, records_ref, response_ref, cell_ref, destination_ref,
                   slot_ref, kept_ref, force_ref, near_ref, far_ref, side_ref, table_ref, total_ref):
    planes, width, lanes = fields_ref.shape[1:]
    rows = planes * width
    particles = records_ref.shape[1]
    for component in range(3):
        plane = fields_ref[component].reshape(rows, lanes).T
        high, low = split(plane, 2)
        table_ref[component * lanes:(component + 1) * lanes, :rows] = high
        table_ref[component * lanes:(component + 1) * lanes, rows:] = low
    groups = 4 * MIG // LANES

    def step(index, sums):
        window = pl.ds(index * chunk, chunk)
        cell = cell_ref[:, window]
        row, lane = divide(cell, lanes)
        row_hot = one_hot(rows, row)
        found = dot(table_ref[...], jnp.concatenate([row_hot, row_hot], axis=0))
        at_lane = sublane_iota(lanes, chunk) == lane
        fluid = jnp.concatenate(
            [jnp.sum(jnp.where(at_lane, found[a * lanes:(a + 1) * lanes], 0.0), axis=0, keepdims=True) for a in range(3)],
            axis=0)
        records = records_ref[:, window]
        speed = records[3:6]
        drag = (fluid - speed) / response_ref[:, window]
        velocity = speed + time_step * drag
        moved = jnp.concatenate([records[0:3] + time_step * velocity, velocity], axis=0)
        live = index * chunk + lax.broadcasted_iota(jnp.int32, (1, chunk), 1) < count_ref[...]
        destination = destination_ref[:, window]
        kept_ref[:, window] = jnp.where(live & (destination == 0), moved, 0.0)
        force_ref[:, window] = jnp.where(live, -coupling * drag, 0.0)
        leaving = live & (destination > 0)
        group, place = divide(slot_ref[:, window], LANES)
        group = jnp.where(leaving, (destination - 1) * (MIG // LANES) + group, -1)
        slot_hot = one_hot(LANES, place)
        padded = jnp.concatenate([moved, jnp.zeros((2, chunk), jnp.float32)], axis=0)
        pieces = []
        for _ in range(2):
            piece = padded.astype(jnp.bfloat16).astype(jnp.float32)
            padded = padded - piece
            pieces += [jnp.where(group == g, piece, 0.0) for g in range(groups)]
        sent = jnp.concatenate(pieces, axis=0).astype(jnp.bfloat16)
        return sums + dot_transposed(sent, slot_hot)

    total_ref[...] = jnp.zeros_like(total_ref)
    if chunk == particles:
        total_ref[...] = step(0, total_ref[...])
    else:
        def loop(index, carry):
            total_ref[...] = step(pl.multiple_of(index, 1), total_ref[...])
            return carry

        lax.fori_loop(0, particles // chunk, loop, 0)
    outgoing = (total_ref[:8 * groups] + total_ref[8 * groups:]).reshape(4, groups // 4, 8, LANES)
    even = lax.rem(row_ref[0], 2) == 0
    near_ref[...] = jnp.where(even, outgoing[0], outgoing[1])
    side_ref[...] = outgoing[2:]
    far_ref[...] = jnp.where(even, outgoing[1], outgoing[0])


def advance(row, counts, fields, records, response, cell, destination, slot):
    planes, width, lanes = fields.shape[1:]
    rows = planes * width
    particles = records.shape[1]
    groups = 4 * MIG // LANES
    box = (groups // 4, 8, LANES)
    return pl.pallas_call(
        functools.partial(advance_kernel, chunk_of(particles, rows)),
        out_shape=(any_space((6, particles)), any_space((3, particles)), any_space(box), any_space(box), any_space((2, *box))),
        in_specs=[SMEM] + [VMEM] * 7,
        out_specs=(VMEM,) * 5,
        scratch_shapes=[pltpu.VMEM((3 * lanes, 2 * rows), jnp.bfloat16), pltpu.VMEM((16 * groups, LANES), jnp.float32)],
        compiler_params=params(40),
        cost_estimate=CHEAP,
        name="advance",
    )(row, counts, fields, records, response, cell, destination, slot)


def along_xy_kernel(chunk, viscous_ref, fields_ref, operator_ref, cell_ref, force_ref, *refs):
    *y_refs, out_ref, total_ref = refs
    if y_refs:
        *y_refs, out_ref, sibling_ref, total_ref = refs
    parts, planes, width, lanes = fields_ref.shape
    rows = planes * width
    half = rows // 2
    particles = cell_ref.shape[1]
    total_ref[...] = jnp.zeros_like(total_ref)

    def step(index):
        window = pl.ds(index * chunk, chunk)
        cell = cell_ref[:, window]
        row, lane = divide(cell, lanes)
        part, row = divide(row, half)
        column = part * lanes + lane
        at_row = is_row(half, row)
        column_hot = one_hot(2 * lanes, column)
        pieces = []
        force = force_ref[:, window]
        for _ in range(2):
            piece = force.astype(jnp.bfloat16)
            force = force - piece.astype(jnp.float32)
            pieces += [jnp.where(at_row, piece[a:a + 1], jnp.bfloat16(0)) for a in range(3)]
        return dot_transposed(jnp.concatenate(pieces, axis=0), column_hot)

    if chunk == particles:
        total_ref[...] = step(0)
    else:
        def loop(index, carry):
            total_ref[...] += step(index)
            return carry

        lax.fori_loop(0, particles // chunk, loop, 0)
    for component in range(parts):
        viscous = viscous_ref[component]
        for plane in range(planes):
            field = fields_ref[component, plane]
            high, low = split(field, 2)
            stacked = jnp.concatenate([high, low, high], axis=0)
            both = dot(operator_ref[...], stacked)
            value = -fields_ref[0, plane] * both[:width] + viscous * both[width:]
            if component < 3:
                for start in range(plane * width, (plane + 1) * width, min(width, half)):
                    part, first = divmod(start, half)
                    size = min(width, half)
                    columns = slice(part * lanes, (part + 1) * lanes)
                    base = component * half + first
                    deposit = (total_ref[base:base + size, columns]
                               + total_ref[3 * half + base:3 * half + base + size, columns])
                    inside = start - plane * width
                    out_ref[component, plane, inside:inside + size] = value[inside:inside + size] + deposit
            else:
                out_ref[component, plane] = value
    if not y_refs:
        return
    row_ref, weight_ref, near_ref, mate_ref, *others = y_refs
    both_ref, diagonal_ref = others
    blocks = [fields_ref, diagonal_ref, both_ref.at[0], both_ref.at[1]]
    size = parts * planes * width
    mine = row_ref[0] * (len(blocks) * planes * 2 * planes * 2)
    step = min(width, 32)
    for component in range(parts):
        for first in range(0, width, step):
            inside = slice(first, first + step)
            sums = [[None] * 2 for _ in range(2 * planes)]
            for index, block in enumerate(blocks):
                for source in range(planes):
                    value = block[component, source, inside]
                    for target in range(2 * planes):
                        for kind in range(2):
                            weight = weight_ref[mine + ((index * planes + source) * 2 * planes + target) * 2 + kind]
                            before = sums[target][kind]
                            sums[target][kind] = weight * value if before is None else before + weight * value
            for plane in range(planes):
                along, curve = sums[plane]
                out_ref[component, plane, inside] += viscous_ref[component] * curve - fields_ref[1, plane, inside] * along
                along, curve = sums[planes + plane]
                row = (component * planes + plane) * width + first
                sibling_ref[row:row + step] = viscous_ref[component] * curve - mate_ref[1, plane, inside] * along
    sibling_ref[size:] = near_ref[...].reshape(MIG // LANES * 8, lanes)


def same_core(block, s):
    return lax.ppermute(block, "row", [(i, i ^ s) for i in range(lax.axis_size("row"))])


def neighbour(row):
    return row ^ 4 if row % 2 else row ^ 2


def along_y_weights(rows, planes):
    deriv = wall_compact(rows * planes)
    operators = np.stack([deriv, deriv @ deriv], axis=-1)
    table = np.zeros((rows, 4, planes, 2, planes, 2), np.float32)
    for me in range(rows):
        for index, other in enumerate((me, me ^ 6, neighbour(me), neighbour(me) ^ 1)):
            for side in range(2):
                target, source = (me ^ side) * planes, other * planes
                block = operators[target:target + planes, source:source + planes]
                table[me, index, :, side] = block.transpose(1, 0, 2)
    return jnp.asarray(table.reshape(-1))


def along_xy(viscous, fields, cell, force, y_part):
    parts, planes, width, lanes = fields.shape
    half = planes * width // 2
    particles = cell.shape[1]
    deriv = periodic_compact(width)
    high, low = two_terms(np.concatenate([deriv, deriv @ deriv], axis=0))
    operator = jnp.asarray(np.concatenate([high, high, low], axis=1))
    specs, outs = [], [any_space(fields.shape)]
    if y_part:
        row, near, mate, others = y_part
        y_part = (row, along_y_weights(lax.axis_size("row"), planes), near, mate, *others)
        specs = [SMEM] * 2 + [VMEM] * (2 + len(others))
        outs.append(any_space((fields.size // lanes + MIG // LANES * 8, lanes)))
    return pl.pallas_call(
        functools.partial(along_xy_kernel, chunk_of(particles, 2 * half)),
        out_shape=tuple(outs),
        in_specs=[SMEM] + [VMEM] * 4 + specs,
        out_specs=(VMEM,) * len(outs),
        scratch_shapes=[pltpu.VMEM((6 * half, 2 * lanes), jnp.float32)],
        compiler_params=params(40),
        cost_estimate=LONG,
        name="along_xy",
    )(viscous, fields, operator, cell, force, *y_part)


def store_kernel(source_ref, target_ref, sem):
    copy = pltpu.make_async_copy(source_ref, target_ref, sem)
    copy.start()
    copy.wait()


def stored(value):
    return pl.pallas_call(
        store_kernel,
        out_shape=any_space(value.shape),
        in_specs=[VMEM],
        out_specs=pl.BlockSpec(memory_space=pl.ANY),
        scratch_shapes=[pltpu.SemaphoreType.DMA(())],
        compiler_params=params(8),
        cost_estimate=CHEAP,
        name="stored",
    )(value)


def along_z_kernel(viscous_ref, high_ref, low_ref, side_ref, *refs):
    count = len(refs) // 2
    blocks, results = refs[:count], refs[count:]
    parts, planes, width, lanes = blocks[0].shape
    rows = parts * planes * width
    pieces = [split(block[...].reshape(rows, lanes), 2) for block in blocks]

    def lines(term):
        return jnp.concatenate(
            [jnp.concatenate([pieces[(d - s) % count][term] for d in range(count)], axis=1) for s in range(count)], axis=0)

    high = lines(0)
    both = dot(high, high_ref[...]) + dot(lines(1), high_ref[...]) + dot(high, low_ref[...])
    for s in range(count):
        speed = blocks[(-s) % count][2]
        for component in range(parts):
            first = s * rows + component * planes * width
            part = both[first:first + planes * width]
            along = part[:, :lanes].reshape(planes, width, lanes)
            curve = part[:, lanes:].reshape(planes, width, lanes)
            value = -speed * along + viscous_ref[component] * curve
            results[s][component * planes * width:(component + 1) * planes * width] = value.reshape(planes * width, lanes)
        row = rows
        for direction in riding(s, count):
            for group in range(side_ref.shape[1]):
                results[s][row:row + 8] = side_ref[direction - 2, group]
                row += 8


def riding(s, count):
    return [direction for direction, step in ((2, 1), (3, -1)) if s == step % count]


def along_z(viscous, side, blocks):
    count = len(blocks)
    shape = blocks[0].shape
    lanes = shape[3]
    points = count * lanes
    deriv = spectral_matrix(points)
    second = deriv @ deriv
    weights = [
        np.concatenate([matrix[d * lanes:(d + 1) * lanes, :lanes].T for matrix in (deriv, second)], axis=1)
        for d in range(count)
    ]
    high, low = two_terms(np.concatenate(weights, axis=0))
    size = int(np.prod(shape))
    return pl.pallas_call(
        along_z_kernel,
        out_shape=tuple(any_space((size // lanes + MIG // LANES * 8 * len(riding(s, count)), lanes)) for s in range(count)),
        in_specs=[SMEM] + [VMEM] * (3 + count),
        out_specs=(VMEM,) * count,
        compiler_params=params(48),
        cost_estimate=CHEAP,
        name="along_z",
    )(viscous, jnp.asarray(high), jnp.asarray(low), side, *blocks)


def pencil_along_y(viscous, fields):
    highest = lax.Precision.HIGHEST
    pencil = lax.all_to_all(fields, "row", split_axis=2, concat_axis=1, tiled=True)
    deriv = wall_compact(pencil.shape[1])
    operators = [jnp.asarray(matrix, jnp.float32) for matrix in (deriv, deriv @ deriv)]
    along, curve = (jnp.einsum("ij,cjxz->cixz", matrix, pencil, precision=highest) for matrix in operators)
    partial = -pencil[1] * along + viscous[:, None, None, None] * curve
    return lax.all_to_all(partial, "row", split_axis=1, concat_axis=2, tiled=True)


def side_kernel(first, *refs):
    blocks, out_ref = refs[:-1], refs[-1]
    for s, block in enumerate(blocks):
        row = first
        for direction in riding(s, len(blocks)):
            for group in range(out_ref.shape[1]):
                out_ref[direction - 2, group] = block[row:row + 8]
                row += 8


def side_particles(blocks):
    first = min(block.shape[0] for block in blocks)
    return pl.pallas_call(
        functools.partial(side_kernel, first),
        out_shape=any_space((2, MIG // LANES, 8, LANES)),
        in_specs=[VMEM] * len(blocks),
        out_specs=VMEM,
        compiler_params=params(8),
        cost_estimate=LONG,
        name="side_particles",
    )(*blocks)


def total_kernel(gathered, row_ref, column_ref, along_x_ref, far_ref, side_ref, near_ref, *refs):
    blocks, out_ref, arrivals_ref = refs[:-2], refs[-2], refs[-1]
    count = len(blocks)
    parts, planes, width, lanes = out_ref.shape
    size = width // count
    whole = parts * planes * width
    for s, block in enumerate(blocks):
        start = pl.multiple_of(lax.rem(column_ref[0] + count - s, count) * size, size)
        rows = pl.ds(start, size)
        for component in range(parts):
            for plane in range(planes):
                first = (component * planes + plane) * size
                value = along_x_ref[component, plane, rows, :] + block[first:first + size]
                if gathered:
                    row = pl.multiple_of((component * planes + plane) * width + start, size)
                    value += near_ref[pl.ds(row, size)]
                out_ref[component, plane, rows, :] = value
    even = lax.rem(row_ref[0], 2) == 0
    for group in range(MIG // LANES):
        columns = slice(group * LANES, (group + 1) * LANES)
        if gathered:
            near = near_ref[whole + group * 8:whole + group * 8 + 6]
        else:
            near = near_ref[group, :6]
        far = far_ref[group, :6]
        arrivals_ref[:, 0, columns] = jnp.where(even, far, near)
        arrivals_ref[:, 1, columns] = jnp.where(even, near, far)
        for direction in (2, 3):
            arrivals_ref[:, direction, columns] = side_ref[direction - 2, group, :6]


def total(gathered, row, column, along_x_part, far, side, near, blocks):
    size = along_x_part.size
    return pl.pallas_call(
        functools.partial(total_kernel, gathered),
        out_shape=(any_space(along_x_part.shape), any_space((6, 4, MIG))),
        in_specs=[SMEM] * 2 + [VMEM] * (4 + len(blocks)),
        out_specs=(VMEM, VMEM),
        compiler_params=params(32),
        cost_estimate=CHEAP,
        name="total",
    )(row, column, along_x_part, far, side, near, *blocks)


def exchange(blocks):
    count = lax.axis_size("col")
    received = list(blocks)
    for s in sorted(range(1, count), key=lambda s: -min(s, count - s)):
        received[s] = lax.ppermute(blocks[s], "col", [(i, (i + s) % count) for i in range(count)])
    return received


def on_device(fields, diffusivity, records, response_time, cell_index, counts, destination, slot):
    rows, columns = lax.axis_size("row"), lax.axis_size("col")
    row, column = lax.axis_index("row"), lax.axis_index("col")
    width = fields.shape[2] // columns
    cell = cell_index.reshape(1, -1)
    blocks = [
        lax.dynamic_slice_in_dim(fields, (column + s) % columns * width, width, axis=2) for s in range(columns)
    ]
    row, column = row.reshape(1), column.reshape(1)
    gathered = rows == 8 and rows * fields.size * 4 <= 16 * MIB
    if gathered:
        mate = same_core(fields, 1)
        mate, blocks = lax.optimization_barrier((mate, blocks))
    lines = exchange(blocks)
    others = []
    if gathered:
        both = jnp.stack([fields, mate])
        later, both = lax.optimization_barrier((fields, both))
        both = lax.ppermute(both, "row", [(i, neighbour(i)) for i in range(rows)])
        others = [both, same_core(later, 6)]
    kept, force, near, far, side = advance(
        row, counts.reshape(1, 1), fields, records, response_time.reshape(1, -1), cell, destination.reshape(1, -1),
        slot.reshape(1, -1))
    side, lines = lax.optimization_barrier((side, lines))
    pairs = [(i, i + 1) for i in range(1, rows - 1, 2)]
    far = lax.ppermute(far, "row", pairs + [(b, a) for a, b in pairs])
    terms_z = exchange(along_z(diffusivity, side, lines))
    terms_x, *near_y = along_xy(diffusivity, fields, cell, force, (row, near, mate, others) if gathered else ())
    kept, terms_x, near_y = lax.optimization_barrier((kept, terms_x, near_y))
    if gathered:
        near = same_core(near_y[0], 1)
    else:
        terms_x = terms_x + pencil_along_y(diffusivity, fields)
        near = lax.ppermute(near, "row", [(i, i ^ 1) for i in range(rows) if i ^ 1 < rows])
    tendency, arrivals = total(gathered, row, column, terms_x, far, side_particles(terms_z), near, terms_z)
    return (tendency, stored(kept), arrivals.transpose(1, 0, 2))


def solution(mesh):
    return jax.shard_map(
        on_device,
        mesh=mesh,
        in_specs=(
            P(None, "row", None, "col"),
            P(),
            P(None, ("row", "col")),
            P(("row", "col")),
            P(("row", "col")),
            P(("row", "col")),
            P(("row", "col")),
            P(("row", "col")),
        ),
        out_specs=(
            P(None, "row", None, "col"),
            P(None, ("row", "col")),
            P(None, None, ("row", "col")),
        ),
        check_vma=False,
    )
```

```python
import functools

import jax
import jax.numpy as jnp
import ml_dtypes
import numpy as np
from jax import lax
from jax.experimental import pallas as pl
from jax.experimental.pallas import tpu as pltpu
from jax.sharding import PartitionSpec as P

MIG = 256
LANES = 128
MIB = 1 << 20

time_step = 0.2
coupling = 0.5
stretch = 1.5


def periodic_compact(points):
    index = np.arange(points)
    offset = (index[None, :] - index[:, None]) % points
    lhs = (offset == 0) + ((offset == 1) | (offset == points - 1)) / 3.0
    rhs = 7.0 / 9.0 * ((offset == 1) * 1.0 - (offset == points - 1))
    rhs = rhs + ((offset == 2) * 1.0 - (offset == points - 2)) / 36.0
    return np.linalg.solve(lhs, rhs)


def wall_compact(points):
    lhs = np.eye(points)
    rhs = np.zeros((points, points))
    for row in range(points):
        if row == 0:
            lhs[0, 1] = 2.0
            rhs[0, :3] = (-2.5, 2.0, 0.5)
        elif row == points - 1:
            lhs[row, row - 1] = 2.0
            rhs[row, -3:] = (-0.5, -2.0, 2.5)
        elif row in (1, points - 2):
            lhs[row, [row - 1, row + 1]] = 0.25
            rhs[row, [row - 1, row + 1]] = (-0.75, 0.75)
        else:
            lhs[row, [row - 1, row + 1]] = 1.0 / 3.0
            rhs[row, [row - 2, row - 1, row + 1, row + 2]] = (-1 / 36, -7 / 9, 7 / 9, 1 / 36)
    coord = -1.0 + 2.0 * np.arange(points) / (points - 1)
    slope = stretch * (1.0 - np.tanh(stretch * coord) ** 2) / np.tanh(stretch)
    return np.linalg.solve(lhs, rhs) / slope[:, None]


def spectral_matrix(points):
    index = np.arange(points)
    offset = index[:, None] - index[None, :]
    parity = 1 - 2 * (offset % 2)
    angle = np.pi * np.where(offset == 0, 1, offset) / points
    return np.where(offset == 0, 0.0, np.pi / points * parity / np.tan(angle))


def two_terms(matrix):
    exact = np.asarray(matrix, np.float32)
    high = exact.astype(ml_dtypes.bfloat16)
    low = (exact - high.astype(np.float32)).astype(ml_dtypes.bfloat16)
    return high, low


def split(value, terms):
    pieces = []
    for _ in range(terms):
        piece = value.astype(jnp.bfloat16)
        pieces.append(piece)
        value = value - piece.astype(jnp.float32)
    return pieces


def dot(a, b):
    return lax.dot_general(a, b, (((1,), (0,)), ((), ())), preferred_element_type=jnp.float32)


def dot_transposed(a, b):
    return lax.dot_general(a, b, (((1,), (1,)), ((), ())), preferred_element_type=jnp.float32)


def sublane_iota(rows, columns, dtype=jnp.int32):
    return lax.broadcasted_iota(dtype, (rows, columns), 0)


def is_row(rows, index):
    return sublane_iota(rows, index.shape[1], jnp.int16) == index.astype(jnp.int16)


def one_hot(rows, index):
    return jnp.where(is_row(rows, index), jnp.bfloat16(1), jnp.bfloat16(0))


def divide(value, by):
    if by & (by - 1):
        return lax.div(value, by), lax.rem(value, by)
    return lax.shift_right_logical(value, by.bit_length() - 1), value & (by - 1)


def chunk_of(particles, rows):
    chunk = particles
    while chunk * rows > 1 << 20 and chunk % 256 == 0:
        chunk //= 2
    return chunk


def params(mib):
    return pltpu.CompilerParams(vmem_limit_bytes=mib * MIB)


CHEAP = pl.CostEstimate(flops=1, bytes_accessed=1, transcendentals=0)
LONG = pl.CostEstimate(flops=20 * 10**9, bytes_accessed=100 * 10**6, transcendentals=0)


def any_space(shape):
    return jax.ShapeDtypeStruct(tuple(shape), jnp.float32)


VMEM = pl.BlockSpec(memory_space=pltpu.VMEM)
SMEM = pl.BlockSpec(memory_space=pltpu.SMEM)


def advance_kernel(chunk, row_ref, count_ref, fields_ref, records_ref, response_ref, cell_ref, destination_ref,
                   slot_ref, kept_ref, force_ref, near_ref, far_ref, side_ref, table_ref, total_ref):
    planes, width, lanes = fields_ref.shape[1:]
    rows = planes * width
    particles = records_ref.shape[1]
    for component in range(3):
        plane = fields_ref[component].reshape(rows, lanes).T
        high, low = split(plane, 2)
        table_ref[component * lanes:(component + 1) * lanes, :rows] = high
        table_ref[component * lanes:(component + 1) * lanes, rows:] = low
    groups = 4 * MIG // LANES

    def step(index, sums):
        window = pl.ds(index * chunk, chunk)
        cell = cell_ref[:, window]
        row, lane = divide(cell, lanes)
        row_hot = one_hot(rows, row)
        found = dot(table_ref[...], jnp.concatenate([row_hot, row_hot], axis=0))
        at_lane = sublane_iota(lanes, chunk) == lane
        fluid = jnp.concatenate(
            [jnp.sum(jnp.where(at_lane, found[a * lanes:(a + 1) * lanes], 0.0), axis=0, keepdims=True) for a in range(3)],
            axis=0)
        records = records_ref[:, window]
        speed = records[3:6]
        drag = (fluid - speed) / response_ref[:, window]
        velocity = speed + time_step * drag
        moved = jnp.concatenate([records[0:3] + time_step * velocity, velocity], axis=0)
        live = index * chunk + lax.broadcasted_iota(jnp.int32, (1, chunk), 1) < count_ref[...]
        destination = destination_ref[:, window]
        kept_ref[:, window] = jnp.where(live & (destination == 0), moved, 0.0)
        force_ref[:, window] = jnp.where(live, -coupling * drag, 0.0)
        leaving = live & (destination > 0)
        group, place = divide(slot_ref[:, window], LANES)
        group = jnp.where(leaving, (destination - 1) * (MIG // LANES) + group, -1)
        slot_hot = one_hot(LANES, place)
        padded = jnp.concatenate([moved, jnp.zeros((2, chunk), jnp.float32)], axis=0)
        pieces = []
        for _ in range(2):
            piece = padded.astype(jnp.bfloat16).astype(jnp.float32)
            padded = padded - piece
            pieces += [jnp.where(group == g, piece, 0.0) for g in range(groups)]
        sent = jnp.concatenate(pieces, axis=0).astype(jnp.bfloat16)
        return sums + dot_transposed(sent, slot_hot)

    total_ref[...] = jnp.zeros_like(total_ref)
    if chunk == particles:
        total_ref[...] = step(0, total_ref[...])
    else:
        def loop(index, carry):
            total_ref[...] = step(pl.multiple_of(index, 1), total_ref[...])
            return carry

        lax.fori_loop(0, particles // chunk, loop, 0)
    outgoing = (total_ref[:8 * groups] + total_ref[8 * groups:]).reshape(4, groups // 4, 8, LANES)
    even = lax.rem(row_ref[0], 2) == 0
    near_ref[...] = jnp.where(even, outgoing[0], outgoing[1])
    side_ref[...] = outgoing[2:]
    far_ref[...] = jnp.where(even, outgoing[1], outgoing[0])


def advance(row, counts, fields, records, response, cell, destination, slot):
    planes, width, lanes = fields.shape[1:]
    rows = planes * width
    particles = records.shape[1]
    groups = 4 * MIG // LANES
    box = (groups // 4, 8, LANES)
    return pl.pallas_call(
        functools.partial(advance_kernel, chunk_of(particles, rows)),
        out_shape=(any_space((6, particles)), any_space((3, particles)), any_space(box), any_space(box), any_space((2, *box))),
        in_specs=[SMEM] + [VMEM] * 7,
        out_specs=(VMEM,) * 5,
        scratch_shapes=[pltpu.VMEM((3 * lanes, 2 * rows), jnp.bfloat16), pltpu.VMEM((16 * groups, LANES), jnp.float32)],
        compiler_params=params(40),
        cost_estimate=CHEAP,
        name="advance",
    )(row, counts, fields, records, response, cell, destination, slot)


def along_xy_kernel(chunk, viscous_ref, fields_ref, operator_ref, cell_ref, force_ref, *refs):
    *y_refs, out_ref, total_ref = refs
    if y_refs:
        *y_refs, out_ref, sibling_ref, total_ref = refs
    parts, planes, width, lanes = fields_ref.shape
    rows = planes * width
    half = rows // 2
    particles = cell_ref.shape[1]
    total_ref[...] = jnp.zeros_like(total_ref)

    def step(index):
        window = pl.ds(index * chunk, chunk)
        cell = cell_ref[:, window]
        row, lane = divide(cell, lanes)
        part, row = divide(row, half)
        column = part * lanes + lane
        at_row = is_row(half, row)
        column_hot = one_hot(2 * lanes, column)
        pieces = []
        force = force_ref[:, window]
        for _ in range(2):
            piece = force.astype(jnp.bfloat16)
            force = force - piece.astype(jnp.float32)
            pieces += [jnp.where(at_row, piece[a:a + 1], jnp.bfloat16(0)) for a in range(3)]
        return dot_transposed(jnp.concatenate(pieces, axis=0), column_hot)

    if chunk == particles:
        total_ref[...] = step(0)
    else:
        def loop(index, carry):
            total_ref[...] += step(index)
            return carry

        lax.fori_loop(0, particles // chunk, loop, 0)
    for component in range(parts):
        viscous = viscous_ref[component]
        for plane in range(planes):
            field = fields_ref[component, plane]
            high, low = split(field, 2)
            stacked = jnp.concatenate([high, low, high], axis=0)
            both = dot(operator_ref[...], stacked)
            value = -fields_ref[0, plane] * both[:width] + viscous * both[width:]
            if component < 3:
                for start in range(plane * width, (plane + 1) * width, min(width, half)):
                    part, first = divmod(start, half)
                    size = min(width, half)
                    columns = slice(part * lanes, (part + 1) * lanes)
                    base = component * half + first
                    deposit = (total_ref[base:base + size, columns]
                               + total_ref[3 * half + base:3 * half + base + size, columns])
                    inside = start - plane * width
                    out_ref[component, plane, inside:inside + size] = value[inside:inside + size] + deposit
            else:
                out_ref[component, plane] = value
    if not y_refs:
        return
    row_ref, weight_ref, near_ref, mate_ref, *others = y_refs
    both_ref, diagonal_ref = others
    blocks = [fields_ref, diagonal_ref, both_ref.at[0], both_ref.at[1]]
    size = parts * planes * width
    mine = row_ref[0] * (len(blocks) * planes * 2 * planes * 2)
    step = min(width, 32)
    for component in range(parts):
        for first in range(0, width, step):
            inside = slice(first, first + step)
            sums = [[None] * 2 for _ in range(2 * planes)]
            for index, block in enumerate(blocks):
                for source in range(planes):
                    value = block[component, source, inside]
                    for target in range(2 * planes):
                        for kind in range(2):
                            weight = weight_ref[mine + ((index * planes + source) * 2 * planes + target) * 2 + kind]
                            before = sums[target][kind]
                            sums[target][kind] = weight * value if before is None else before + weight * value
            for plane in range(planes):
                along, curve = sums[plane]
                out_ref[component, plane, inside] += viscous_ref[component] * curve - fields_ref[1, plane, inside] * along
                along, curve = sums[planes + plane]
                row = (component * planes + plane) * width + first
                sibling_ref[row:row + step] = viscous_ref[component] * curve - mate_ref[1, plane, inside] * along
    sibling_ref[size:] = near_ref[...].reshape(MIG // LANES * 8, lanes)


def same_core(block, s):
    return lax.ppermute(block, "row", [(i, i ^ s) for i in range(lax.axis_size("row"))])


def neighbour(row):
    return row ^ 4 if row % 2 else row ^ 2


def along_y_weights(rows, planes):
    deriv = wall_compact(rows * planes)
    operators = np.stack([deriv, deriv @ deriv], axis=-1)
    table = np.zeros((rows, 4, planes, 2, planes, 2), np.float32)
    for me in range(rows):
        for index, other in enumerate((me, me ^ 6, neighbour(me), neighbour(me) ^ 1)):
            for side in range(2):
                target, source = (me ^ side) * planes, other * planes
                block = operators[target:target + planes, source:source + planes]
                table[me, index, :, side] = block.transpose(1, 0, 2)
    return jnp.asarray(table.reshape(-1))


def along_xy(viscous, fields, cell, force, y_part):
    parts, planes, width, lanes = fields.shape
    half = planes * width // 2
    particles = cell.shape[1]
    deriv = periodic_compact(width)
    high, low = two_terms(np.concatenate([deriv, deriv @ deriv], axis=0))
    operator = jnp.asarray(np.concatenate([high, high, low], axis=1))
    specs, outs = [], [any_space(fields.shape)]
    if y_part:
        row, near, mate, others = y_part
        y_part = (row, along_y_weights(lax.axis_size("row"), planes), near, mate, *others)
        specs = [SMEM] * 2 + [VMEM] * (2 + len(others))
        outs.append(any_space((fields.size // lanes + MIG // LANES * 8, lanes)))
    return pl.pallas_call(
        functools.partial(along_xy_kernel, chunk_of(particles, 2 * half)),
        out_shape=tuple(outs),
        in_specs=[SMEM] + [VMEM] * 4 + specs,
        out_specs=(VMEM,) * len(outs),
        scratch_shapes=[pltpu.VMEM((6 * half, 2 * lanes), jnp.float32)],
        compiler_params=params(40),
        cost_estimate=LONG,
        name="along_xy",
    )(viscous, fields, operator, cell, force, *y_part)


def store_kernel(source_ref, target_ref, sem):
    copy = pltpu.make_async_copy(source_ref, target_ref, sem)
    copy.start()
    copy.wait()


def stored(value):
    return pl.pallas_call(
        store_kernel,
        out_shape=any_space(value.shape),
        in_specs=[VMEM],
        out_specs=pl.BlockSpec(memory_space=pl.ANY),
        scratch_shapes=[pltpu.SemaphoreType.DMA(())],
        compiler_params=params(8),
        cost_estimate=CHEAP,
        name="stored",
    )(value)


def along_z_kernel(diffusivity_ref, high_ref, low_ref, side_ref, *refs):
    *refs, viscous_ref, viscous_sem = refs
    fetch = pltpu.make_async_copy(diffusivity_ref, viscous_ref, viscous_sem)
    fetch.start()
    count = len(refs) // 2
    blocks, results = refs[:count], refs[count:]
    parts, planes, width, lanes = blocks[0].shape
    rows = parts * planes * width
    pieces = [split(block[...].reshape(rows, lanes), 2) for block in blocks]

    def lines(term):
        return jnp.concatenate(
            [jnp.concatenate([pieces[(d - s) % count][term] for d in range(count)], axis=1) for s in range(count)], axis=0)

    high = lines(0)
    both = dot(high, high_ref[...]) + dot(lines(1), high_ref[...]) + dot(high, low_ref[...])
    fetch.wait()
    for s in range(count):
        speed = blocks[(-s) % count][2]
        for component in range(parts):
            first = s * rows + component * planes * width
            part = both[first:first + planes * width]
            along = part[:, :lanes].reshape(planes, width, lanes)
            curve = part[:, lanes:].reshape(planes, width, lanes)
            value = -speed * along + viscous_ref[component] * curve
            results[s][component * planes * width:(component + 1) * planes * width] = value.reshape(planes * width, lanes)
        row = rows
        for direction in riding(s, count):
            for group in range(side_ref.shape[1]):
                results[s][row:row + 8] = side_ref[direction - 2, group]
                row += 8


def riding(s, count):
    return [direction for direction, step in ((2, 1), (3, -1)) if s == step % count]


def along_z(viscous, side, blocks):
    count = len(blocks)
    shape = blocks[0].shape
    lanes = shape[3]
    points = count * lanes
    deriv = spectral_matrix(points)
    second = deriv @ deriv
    weights = [
        np.concatenate([matrix[d * lanes:(d + 1) * lanes, :lanes].T for matrix in (deriv, second)], axis=1)
        for d in range(count)
    ]
    high, low = two_terms(np.concatenate(weights, axis=0))
    size = int(np.prod(shape))
    return pl.pallas_call(
        along_z_kernel,
        out_shape=tuple(any_space((size // lanes + MIG // LANES * 8 * len(riding(s, count)), lanes)) for s in range(count)),
        in_specs=[pl.BlockSpec(memory_space=pl.ANY)] + [VMEM] * (3 + count),
        out_specs=(VMEM,) * count,
        scratch_shapes=[pltpu.SMEM(viscous.shape, jnp.float32), pltpu.SemaphoreType.DMA(())],
        compiler_params=params(48),
        cost_estimate=CHEAP,
        name="along_z",
    )(viscous, jnp.asarray(high), jnp.asarray(low), side, *blocks)


def pencil_along_y(viscous, fields):
    highest = lax.Precision.HIGHEST
    pencil = lax.all_to_all(fields, "row", split_axis=2, concat_axis=1, tiled=True)
    deriv = wall_compact(pencil.shape[1])
    operators = [jnp.asarray(matrix, jnp.float32) for matrix in (deriv, deriv @ deriv)]
    along, curve = (jnp.einsum("ij,cjxz->cixz", matrix, pencil, precision=highest) for matrix in operators)
    partial = -pencil[1] * along + viscous[:, None, None, None] * curve
    return lax.all_to_all(partial, "row", split_axis=1, concat_axis=2, tiled=True)


def side_kernel(first, *refs):
    blocks, out_ref = refs[:-1], refs[-1]
    for s, block in enumerate(blocks):
        row = first
        for direction in riding(s, len(blocks)):
            for group in range(out_ref.shape[1]):
                out_ref[direction - 2, group] = block[row:row + 8]
                row += 8


def side_particles(blocks):
    first = min(block.shape[0] for block in blocks)
    return pl.pallas_call(
        functools.partial(side_kernel, first),
        out_shape=any_space((2, MIG // LANES, 8, LANES)),
        in_specs=[VMEM] * len(blocks),
        out_specs=VMEM,
        compiler_params=params(8),
        cost_estimate=LONG,
        name="side_particles",
    )(*blocks)


def total_kernel(gathered, row_ref, column_ref, along_x_ref, far_ref, side_ref, near_ref, *refs):
    blocks, out_ref, arrivals_ref = refs[:-2], refs[-2], refs[-1]
    count = len(blocks)
    parts, planes, width, lanes = out_ref.shape
    size = width // count
    whole = parts * planes * width
    for s, block in enumerate(blocks):
        start = pl.multiple_of(lax.rem(column_ref[0] + count - s, count) * size, size)
        rows = pl.ds(start, size)
        for component in range(parts):
            for plane in range(planes):
                first = (component * planes + plane) * size
                value = along_x_ref[component, plane, rows, :] + block[first:first + size]
                if gathered:
                    row = pl.multiple_of((component * planes + plane) * width + start, size)
                    value += near_ref[pl.ds(row, size)]
                out_ref[component, plane, rows, :] = value
    even = lax.rem(row_ref[0], 2) == 0
    for group in range(MIG // LANES):
        columns = slice(group * LANES, (group + 1) * LANES)
        if gathered:
            near = near_ref[whole + group * 8:whole + group * 8 + 6]
        else:
            near = near_ref[group, :6]
        far = far_ref[group, :6]
        arrivals_ref[:, 0, columns] = jnp.where(even, far, near)
        arrivals_ref[:, 1, columns] = jnp.where(even, near, far)
        for direction in (2, 3):
            arrivals_ref[:, direction, columns] = side_ref[direction - 2, group, :6]


def total(gathered, row, column, along_x_part, far, side, near, blocks):
    size = along_x_part.size
    return pl.pallas_call(
        functools.partial(total_kernel, gathered),
        out_shape=(any_space(along_x_part.shape), any_space((6, 4, MIG))),
        in_specs=[SMEM] * 2 + [VMEM] * (4 + len(blocks)),
        out_specs=(VMEM, VMEM),
        compiler_params=params(32),
        cost_estimate=CHEAP,
        name="total",
    )(row, column, along_x_part, far, side, near, *blocks)


def exchange(blocks):
    count = lax.axis_size("col")
    received = list(blocks)
    for s in sorted(range(1, count), key=lambda s: -min(s, count - s)):
        received[s] = lax.ppermute(blocks[s], "col", [(i, (i + s) % count) for i in range(count)])
    return received


def on_device(fields, diffusivity, records, response_time, cell_index, counts, destination, slot):
    rows, columns = lax.axis_size("row"), lax.axis_size("col")
    row, column = lax.axis_index("row"), lax.axis_index("col")
    width = fields.shape[2] // columns
    cell = cell_index.reshape(1, -1)
    blocks = [
        lax.dynamic_slice_in_dim(fields, (column + s) % columns * width, width, axis=2) for s in range(columns)
    ]
    row, column = row.reshape(1), column.reshape(1)
    gathered = rows == 8 and rows * fields.size * 4 <= 16 * MIB
    if gathered:
        mate = same_core(fields, 1)
        mate, blocks = lax.optimization_barrier((mate, blocks))
    lines = exchange(blocks)
    others = []
    if gathered:
        both = jnp.stack([fields, mate])
        later, both = lax.optimization_barrier((fields, both))
        both = lax.ppermute(both, "row", [(i, neighbour(i)) for i in range(rows)])
        others = [both, same_core(later, 6)]
    kept, force, near, far, side = advance(
        row, counts.reshape(1, 1), fields, records, response_time.reshape(1, -1), cell, destination.reshape(1, -1),
        slot.reshape(1, -1))
    side, lines = lax.optimization_barrier((side, lines))
    pairs = [(i, i + 1) for i in range(1, rows - 1, 2)]
    far = lax.ppermute(far, "row", pairs + [(b, a) for a, b in pairs])
    terms_z = exchange(along_z(diffusivity, side, lines))
    terms_x, *near_y = along_xy(diffusivity, fields, cell, force, (row, near, mate, others) if gathered else ())
    kept, terms_x, near_y = lax.optimization_barrier((kept, terms_x, near_y))
    if gathered:
        near = same_core(near_y[0], 1)
    else:
        terms_x = terms_x + pencil_along_y(diffusivity, fields)
        near = lax.ppermute(near, "row", [(i, i ^ 1) for i in range(rows) if i ^ 1 < rows])
    tendency, arrivals = total(gathered, row, column, terms_x, far, side_particles(terms_z), near, terms_z)
    return (tendency, stored(kept), arrivals.transpose(1, 0, 2))


def solution(mesh):
    return jax.shard_map(
        on_device,
        mesh=mesh,
        in_specs=(
            P(None, "row", None, "col"),
            P(),
            P(None, ("row", "col")),
            P(("row", "col")),
            P(("row", "col")),
            P(("row", "col")),
            P(("row", "col")),
            P(("row", "col")),
        ),
        out_specs=(
            P(None, "row", None, "col"),
            P(None, ("row", "col")),
            P(None, None, ("row", "col")),
        ),
        check_vma=False,
    )
```

```python
import functools

import jax
import jax.numpy as jnp
import ml_dtypes
import numpy as np
from jax import lax
from jax.experimental import pallas as pl
from jax.experimental.pallas import tpu as pltpu
from jax.sharding import PartitionSpec as P

MIG = 256
LANES = 128
MIB = 1 << 20

time_step = 0.2
coupling = 0.5
stretch = 1.5


def periodic_compact(points):
    index = np.arange(points)
    offset = (index[None, :] - index[:, None]) % points
    lhs = (offset == 0) + ((offset == 1) | (offset == points - 1)) / 3.0
    rhs = 7.0 / 9.0 * ((offset == 1) * 1.0 - (offset == points - 1))
    rhs = rhs + ((offset == 2) * 1.0 - (offset == points - 2)) / 36.0
    return np.linalg.solve(lhs, rhs)


def wall_compact(points):
    lhs = np.eye(points)
    rhs = np.zeros((points, points))
    for row in range(points):
        if row == 0:
            lhs[0, 1] = 2.0
            rhs[0, :3] = (-2.5, 2.0, 0.5)
        elif row == points - 1:
            lhs[row, row - 1] = 2.0
            rhs[row, -3:] = (-0.5, -2.0, 2.5)
        elif row in (1, points - 2):
            lhs[row, [row - 1, row + 1]] = 0.25
            rhs[row, [row - 1, row + 1]] = (-0.75, 0.75)
        else:
            lhs[row, [row - 1, row + 1]] = 1.0 / 3.0
            rhs[row, [row - 2, row - 1, row + 1, row + 2]] = (-1 / 36, -7 / 9, 7 / 9, 1 / 36)
    coord = -1.0 + 2.0 * np.arange(points) / (points - 1)
    slope = stretch * (1.0 - np.tanh(stretch * coord) ** 2) / np.tanh(stretch)
    return np.linalg.solve(lhs, rhs) / slope[:, None]


def spectral_matrix(points):
    index = np.arange(points)
    offset = index[:, None] - index[None, :]
    parity = 1 - 2 * (offset % 2)
    angle = np.pi * np.where(offset == 0, 1, offset) / points
    return np.where(offset == 0, 0.0, np.pi / points * parity / np.tan(angle))


def two_terms(matrix):
    exact = np.asarray(matrix, np.float32)
    high = exact.astype(ml_dtypes.bfloat16)
    low = (exact - high.astype(np.float32)).astype(ml_dtypes.bfloat16)
    return high, low


def split(value, terms):
    pieces = []
    for _ in range(terms):
        piece = value.astype(jnp.bfloat16)
        pieces.append(piece)
        value = value - piece.astype(jnp.float32)
    return pieces


def dot(a, b):
    return lax.dot_general(a, b, (((1,), (0,)), ((), ())), preferred_element_type=jnp.float32)


def dot_transposed(a, b):
    return lax.dot_general(a, b, (((1,), (1,)), ((), ())), preferred_element_type=jnp.float32)


def sublane_iota(rows, columns, dtype=jnp.int32):
    return lax.broadcasted_iota(dtype, (rows, columns), 0)


def is_row(rows, index):
    return sublane_iota(rows, index.shape[1], jnp.int16) == index.astype(jnp.int16)


def one_hot(rows, index):
    return jnp.where(is_row(rows, index), jnp.bfloat16(1), jnp.bfloat16(0))


def divide(value, by):
    if by & (by - 1):
        return lax.div(value, by), lax.rem(value, by)
    return lax.shift_right_logical(value, by.bit_length() - 1), value & (by - 1)


def chunk_of(particles, rows):
    chunk = particles
    while chunk * rows > 1 << 20 and chunk % 256 == 0:
        chunk //= 2
    return chunk


def params(mib):
    return pltpu.CompilerParams(vmem_limit_bytes=mib * MIB)


CHEAP = pl.CostEstimate(flops=1, bytes_accessed=1, transcendentals=0)
LONG = pl.CostEstimate(flops=20 * 10**9, bytes_accessed=100 * 10**6, transcendentals=0)


def any_space(shape):
    return jax.ShapeDtypeStruct(tuple(shape), jnp.float32)


VMEM = pl.BlockSpec(memory_space=pltpu.VMEM)
SMEM = pl.BlockSpec(memory_space=pltpu.SMEM)


def advance_kernel(chunk, row_ref, count_ref, fields_ref, records_ref, response_ref, cell_ref, destination_ref,
                   slot_ref, kept_ref, force_ref, near_ref, far_ref, side_ref, table_ref, total_ref):
    planes, width, lanes = fields_ref.shape[1:]
    rows = planes * width
    particles = records_ref.shape[1]
    for component in range(3):
        plane = fields_ref[component].reshape(rows, lanes).T
        high, low = split(plane, 2)
        table_ref[component * lanes:(component + 1) * lanes, :rows] = high
        table_ref[component * lanes:(component + 1) * lanes, rows:] = low
    groups = 4 * MIG // LANES

    def step(index, sums):
        window = pl.ds(index * chunk, chunk)
        cell = cell_ref[:, window]
        row, lane = divide(cell, lanes)
        row_hot = one_hot(rows, row)
        found = dot(table_ref[...], jnp.concatenate([row_hot, row_hot], axis=0))
        at_lane = sublane_iota(lanes, chunk) == lane
        fluid = jnp.concatenate(
            [jnp.sum(jnp.where(at_lane, found[a * lanes:(a + 1) * lanes], 0.0), axis=0, keepdims=True) for a in range(3)],
            axis=0)
        records = records_ref[:, window]
        speed = records[3:6]
        drag = (fluid - speed) / response_ref[:, window]
        velocity = speed + time_step * drag
        moved = jnp.concatenate([records[0:3] + time_step * velocity, velocity], axis=0)
        live = index * chunk + lax.broadcasted_iota(jnp.int32, (1, chunk), 1) < count_ref[...]
        destination = destination_ref[:, window]
        kept_ref[:, window] = jnp.where(live & (destination == 0), moved, 0.0)
        force_ref[:, window] = jnp.where(live, -coupling * drag, 0.0)
        leaving = live & (destination > 0)
        group, place = divide(slot_ref[:, window], LANES)
        group = jnp.where(leaving, (destination - 1) * (MIG // LANES) + group, -1)
        slot_hot = one_hot(LANES, place)
        padded = jnp.concatenate([moved, jnp.zeros((2, chunk), jnp.float32)], axis=0)
        pieces = []
        for _ in range(2):
            piece = padded.astype(jnp.bfloat16).astype(jnp.float32)
            padded = padded - piece
            pieces += [jnp.where(group == g, piece, 0.0) for g in range(groups)]
        sent = jnp.concatenate(pieces, axis=0).astype(jnp.bfloat16)
        return sums + dot_transposed(sent, slot_hot)

    total_ref[...] = jnp.zeros_like(total_ref)
    if chunk == particles:
        total_ref[...] = step(0, total_ref[...])
    else:
        def loop(index, carry):
            total_ref[...] = step(pl.multiple_of(index, 1), total_ref[...])
            return carry

        lax.fori_loop(0, particles // chunk, loop, 0)
    outgoing = (total_ref[:8 * groups] + total_ref[8 * groups:]).reshape(4, groups // 4, 8, LANES)
    even = lax.rem(row_ref[0], 2) == 0
    near_ref[...] = jnp.where(even, outgoing[0], outgoing[1])
    side_ref[...] = outgoing[2:]
    far_ref[...] = jnp.where(even, outgoing[1], outgoing[0])


def advance(row, counts, fields, records, response, cell, destination, slot):
    planes, width, lanes = fields.shape[1:]
    rows = planes * width
    particles = records.shape[1]
    groups = 4 * MIG // LANES
    box = (groups // 4, 8, LANES)
    return pl.pallas_call(
        functools.partial(advance_kernel, chunk_of(particles, rows)),
        out_shape=(any_space((6, particles)), any_space((3, particles)), any_space(box), any_space(box), any_space((2, *box))),
        in_specs=[SMEM] + [VMEM] * 7,
        out_specs=(VMEM,) * 5,
        scratch_shapes=[pltpu.VMEM((3 * lanes, 2 * rows), jnp.bfloat16), pltpu.VMEM((16 * groups, LANES), jnp.float32)],
        compiler_params=params(40),
        cost_estimate=CHEAP,
        name="advance",
    )(row, counts, fields, records, response, cell, destination, slot)


def along_xy_kernel(chunk, diffusivity_ref, fields_ref, operator_ref, cell_ref, force_ref, *refs):
    *refs, viscous_ref, weight_ref, sems = refs
    fetches = [pltpu.make_async_copy(diffusivity_ref, viscous_ref, sems.at[0])]
    if len(refs) > 2:
        fetches.append(pltpu.make_async_copy(refs[1], weight_ref, sems.at[1]))
    for fetch in fetches:
        fetch.start()
    *y_refs, out_ref, total_ref = refs
    if y_refs:
        *y_refs, out_ref, sibling_ref, total_ref = refs
    parts, planes, width, lanes = fields_ref.shape
    rows = planes * width
    half = rows // 2
    particles = cell_ref.shape[1]
    total_ref[...] = jnp.zeros_like(total_ref)

    def step(index):
        window = pl.ds(index * chunk, chunk)
        cell = cell_ref[:, window]
        row, lane = divide(cell, lanes)
        part, row = divide(row, half)
        column = part * lanes + lane
        at_row = is_row(half, row)
        column_hot = one_hot(2 * lanes, column)
        pieces = []
        force = force_ref[:, window]
        for _ in range(2):
            piece = force.astype(jnp.bfloat16)
            force = force - piece.astype(jnp.float32)
            pieces += [jnp.where(at_row, piece[a:a + 1], jnp.bfloat16(0)) for a in range(3)]
        return dot_transposed(jnp.concatenate(pieces, axis=0), column_hot)

    if chunk == particles:
        total_ref[...] = step(0)
    else:
        def loop(index, carry):
            total_ref[...] += step(index)
            return carry

        lax.fori_loop(0, particles // chunk, loop, 0)
    for fetch in fetches:
        fetch.wait()
    for component in range(parts):
        viscous = viscous_ref[component]
        for plane in range(planes):
            field = fields_ref[component, plane]
            high, low = split(field, 2)
            stacked = jnp.concatenate([high, low, high], axis=0)
            both = dot(operator_ref[...], stacked)
            value = -fields_ref[0, plane] * both[:width] + viscous * both[width:]
            if component < 3:
                for start in range(plane * width, (plane + 1) * width, min(width, half)):
                    part, first = divmod(start, half)
                    size = min(width, half)
                    columns = slice(part * lanes, (part + 1) * lanes)
                    base = component * half + first
                    deposit = (total_ref[base:base + size, columns]
                               + total_ref[3 * half + base:3 * half + base + size, columns])
                    inside = start - plane * width
                    out_ref[component, plane, inside:inside + size] = value[inside:inside + size] + deposit
            else:
                out_ref[component, plane] = value
    if not y_refs:
        return
    row_ref, _, near_ref, mate_ref, *others = y_refs
    both_ref, diagonal_ref = others
    blocks = [fields_ref, diagonal_ref, both_ref.at[0], both_ref.at[1]]
    size = parts * planes * width
    mine = row_ref[0] * (len(blocks) * planes * 2 * planes * 2)
    step = min(width, 32)
    for component in range(parts):
        for first in range(0, width, step):
            inside = slice(first, first + step)
            sums = [[None] * 2 for _ in range(2 * planes)]
            for index, block in enumerate(blocks):
                for source in range(planes):
                    value = block[component, source, inside]
                    for target in range(2 * planes):
                        for kind in range(2):
                            weight = weight_ref[mine + ((index * planes + source) * 2 * planes + target) * 2 + kind]
                            before = sums[target][kind]
                            sums[target][kind] = weight * value if before is None else before + weight * value
            for plane in range(planes):
                along, curve = sums[plane]
                out_ref[component, plane, inside] += viscous_ref[component] * curve - fields_ref[1, plane, inside] * along
                along, curve = sums[planes + plane]
                row = (component * planes + plane) * width + first
                sibling_ref[row:row + step] = viscous_ref[component] * curve - mate_ref[1, plane, inside] * along
    sibling_ref[size:] = near_ref[...].reshape(MIG // LANES * 8, lanes)


def same_core(block, s):
    return lax.ppermute(block, "row", [(i, i ^ s) for i in range(lax.axis_size("row"))])


def neighbour(row):
    return row ^ 4 if row % 2 else row ^ 2


def along_y_weights(rows, planes):
    deriv = wall_compact(rows * planes)
    operators = np.stack([deriv, deriv @ deriv], axis=-1)
    table = np.zeros((rows, 4, planes, 2, planes, 2), np.float32)
    for me in range(rows):
        for index, other in enumerate((me, me ^ 6, neighbour(me), neighbour(me) ^ 1)):
            for side in range(2):
                target, source = (me ^ side) * planes, other * planes
                block = operators[target:target + planes, source:source + planes]
                table[me, index, :, side] = block.transpose(1, 0, 2)
    return jnp.asarray(table.reshape(-1))


def along_xy(viscous, fields, cell, force, y_part):
    parts, planes, width, lanes = fields.shape
    half = planes * width // 2
    particles = cell.shape[1]
    deriv = periodic_compact(width)
    high, low = two_terms(np.concatenate([deriv, deriv @ deriv], axis=0))
    operator = jnp.asarray(np.concatenate([high, high, low], axis=1))
    specs, outs = [], [any_space(fields.shape)]
    if y_part:
        row, near, mate, others = y_part
        y_part = (row, along_y_weights(lax.axis_size("row"), planes), near, mate, *others)
        specs = [SMEM, pl.BlockSpec(memory_space=pl.ANY)] + [VMEM] * (2 + len(others))
        outs.append(any_space((fields.size // lanes + MIG // LANES * 8, lanes)))
    return pl.pallas_call(
        functools.partial(along_xy_kernel, chunk_of(particles, 2 * half)),
        out_shape=tuple(outs),
        in_specs=[pl.BlockSpec(memory_space=pl.ANY)] + [VMEM] * 4 + specs,
        out_specs=(VMEM,) * len(outs),
        scratch_shapes=[
            pltpu.VMEM((6 * half, 2 * lanes), jnp.float32), pltpu.SMEM(viscous.shape, jnp.float32),
            pltpu.SMEM(y_part[1].shape if y_part else (LANES,), jnp.float32), pltpu.SemaphoreType.DMA((2,))],
        compiler_params=params(40),
        cost_estimate=LONG,
        name="along_xy",
    )(viscous, fields, operator, cell, force, *y_part)


def store_kernel(source_ref, target_ref, sem):
    copy = pltpu.make_async_copy(source_ref, target_ref, sem)
    copy.start()
    copy.wait()


def stored(value):
    return pl.pallas_call(
        store_kernel,
        out_shape=any_space(value.shape),
        in_specs=[VMEM],
        out_specs=pl.BlockSpec(memory_space=pl.ANY),
        scratch_shapes=[pltpu.SemaphoreType.DMA(())],
        compiler_params=params(8),
        cost_estimate=CHEAP,
        name="stored",
    )(value)


def along_z_kernel(diffusivity_ref, high_ref, low_ref, side_ref, *refs):
    *refs, viscous_ref, viscous_sem = refs
    fetch = pltpu.make_async_copy(diffusivity_ref, viscous_ref, viscous_sem)
    fetch.start()
    count = len(refs) // 2
    blocks, results = refs[:count], refs[count:]
    parts, planes, width, lanes = blocks[0].shape
    rows = parts * planes * width
    pieces = [split(block[...].reshape(rows, lanes), 2) for block in blocks]

    def lines(term):
        return jnp.concatenate(
            [jnp.concatenate([pieces[(d - s) % count][term] for d in range(count)], axis=1) for s in range(count)], axis=0)

    high = lines(0)
    both = dot(high, high_ref[...]) + dot(lines(1), high_ref[...]) + dot(high, low_ref[...])
    fetch.wait()
    for s in range(count):
        speed = blocks[(-s) % count][2]
        for component in range(parts):
            first = s * rows + component * planes * width
            part = both[first:first + planes * width]
            along = part[:, :lanes].reshape(planes, width, lanes)
            curve = part[:, lanes:].reshape(planes, width, lanes)
            value = -speed * along + viscous_ref[component] * curve
            results[s][component * planes * width:(component + 1) * planes * width] = value.reshape(planes * width, lanes)
        row = rows
        for direction in riding(s, count):
            for group in range(side_ref.shape[1]):
                results[s][row:row + 8] = side_ref[direction - 2, group]
                row += 8


def riding(s, count):
    return [direction for direction, step in ((2, 1), (3, -1)) if s == step % count]


def along_z(viscous, side, blocks):
    count = len(blocks)
    shape = blocks[0].shape
    lanes = shape[3]
    points = count * lanes
    deriv = spectral_matrix(points)
    second = deriv @ deriv
    weights = [
        np.concatenate([matrix[d * lanes:(d + 1) * lanes, :lanes].T for matrix in (deriv, second)], axis=1)
        for d in range(count)
    ]
    high, low = two_terms(np.concatenate(weights, axis=0))
    size = int(np.prod(shape))
    return pl.pallas_call(
        along_z_kernel,
        out_shape=tuple(any_space((size // lanes + MIG // LANES * 8 * len(riding(s, count)), lanes)) for s in range(count)),
        in_specs=[pl.BlockSpec(memory_space=pl.ANY)] + [VMEM] * (3 + count),
        out_specs=(VMEM,) * count,
        scratch_shapes=[pltpu.SMEM(viscous.shape, jnp.float32), pltpu.SemaphoreType.DMA(())],
        compiler_params=params(48),
        cost_estimate=CHEAP,
        name="along_z",
    )(viscous, jnp.asarray(high), jnp.asarray(low), side, *blocks)


def pencil_along_y(viscous, fields):
    highest = lax.Precision.HIGHEST
    pencil = lax.all_to_all(fields, "row", split_axis=2, concat_axis=1, tiled=True)
    deriv = wall_compact(pencil.shape[1])
    operators = [jnp.asarray(matrix, jnp.float32) for matrix in (deriv, deriv @ deriv)]
    along, curve = (jnp.einsum("ij,cjxz->cixz", matrix, pencil, precision=highest) for matrix in operators)
    partial = -pencil[1] * along + viscous[:, None, None, None] * curve
    return lax.all_to_all(partial, "row", split_axis=1, concat_axis=2, tiled=True)


def side_kernel(first, *refs):
    blocks, out_ref = refs[:-1], refs[-1]
    for s, block in enumerate(blocks):
        row = first
        for direction in riding(s, len(blocks)):
            for group in range(out_ref.shape[1]):
                out_ref[direction - 2, group] = block[row:row + 8]
                row += 8


def side_particles(blocks):
    first = min(block.shape[0] for block in blocks)
    return pl.pallas_call(
        functools.partial(side_kernel, first),
        out_shape=any_space((2, MIG // LANES, 8, LANES)),
        in_specs=[VMEM] * len(blocks),
        out_specs=VMEM,
        compiler_params=params(8),
        cost_estimate=LONG,
        name="side_particles",
    )(*blocks)


def total_kernel(gathered, row_ref, column_ref, along_x_ref, far_ref, side_ref, near_ref, *refs):
    blocks, out_ref, arrivals_ref = refs[:-2], refs[-2], refs[-1]
    count = len(blocks)
    parts, planes, width, lanes = out_ref.shape
    size = width // count
    whole = parts * planes * width
    for s, block in enumerate(blocks):
        start = pl.multiple_of(lax.rem(column_ref[0] + count - s, count) * size, size)
        rows = pl.ds(start, size)
        for component in range(parts):
            for plane in range(planes):
                first = (component * planes + plane) * size
                value = along_x_ref[component, plane, rows, :] + block[first:first + size]
                if gathered:
                    row = pl.multiple_of((component * planes + plane) * width + start, size)
                    value += near_ref[pl.ds(row, size)]
                out_ref[component, plane, rows, :] = value
    even = lax.rem(row_ref[0], 2) == 0
    for group in range(MIG // LANES):
        columns = slice(group * LANES, (group + 1) * LANES)
        if gathered:
            near = near_ref[whole + group * 8:whole + group * 8 + 6]
        else:
            near = near_ref[group, :6]
        far = far_ref[group, :6]
        arrivals_ref[:, 0, columns] = jnp.where(even, far, near)
        arrivals_ref[:, 1, columns] = jnp.where(even, near, far)
        for direction in (2, 3):
            arrivals_ref[:, direction, columns] = side_ref[direction - 2, group, :6]


def total(gathered, row, column, along_x_part, far, side, near, blocks):
    size = along_x_part.size
    return pl.pallas_call(
        functools.partial(total_kernel, gathered),
        out_shape=(any_space(along_x_part.shape), any_space((6, 4, MIG))),
        in_specs=[SMEM] * 2 + [VMEM] * (4 + len(blocks)),
        out_specs=(VMEM, VMEM),
        compiler_params=params(32),
        cost_estimate=CHEAP,
        name="total",
    )(row, column, along_x_part, far, side, near, *blocks)


def exchange(blocks):
    count = lax.axis_size("col")
    received = list(blocks)
    for s in sorted(range(1, count), key=lambda s: -min(s, count - s)):
        received[s] = lax.ppermute(blocks[s], "col", [(i, (i + s) % count) for i in range(count)])
    return received


def on_device(fields, diffusivity, records, response_time, cell_index, counts, destination, slot):
    rows, columns = lax.axis_size("row"), lax.axis_size("col")
    row, column = lax.axis_index("row"), lax.axis_index("col")
    width = fields.shape[2] // columns
    cell = cell_index.reshape(1, -1)
    blocks = [
        lax.dynamic_slice_in_dim(fields, (column + s) % columns * width, width, axis=2) for s in range(columns)
    ]
    row, column = row.reshape(1), column.reshape(1)
    gathered = rows == 8 and rows * fields.size * 4 <= 16 * MIB
    if gathered:
        mate = same_core(fields, 1)
        mate, blocks = lax.optimization_barrier((mate, blocks))
    lines = exchange(blocks)
    others = []
    if gathered:
        both = jnp.stack([fields, mate])
        later, both = lax.optimization_barrier((fields, both))
        both = lax.ppermute(both, "row", [(i, neighbour(i)) for i in range(rows)])
        others = [both, same_core(later, 6)]
    kept, force, near, far, side = advance(
        row, counts.reshape(1, 1), fields, records, response_time.reshape(1, -1), cell, destination.reshape(1, -1),
        slot.reshape(1, -1))
    side, lines = lax.optimization_barrier((side, lines))
    pairs = [(i, i + 1) for i in range(1, rows - 1, 2)]
    far = lax.ppermute(far, "row", pairs + [(b, a) for a, b in pairs])
    terms_z = exchange(along_z(diffusivity, side, lines))
    terms_x, *near_y = along_xy(diffusivity, fields, cell, force, (row, near, mate, others) if gathered else ())
    kept, terms_x, near_y = lax.optimization_barrier((kept, terms_x, near_y))
    if gathered:
        near = same_core(near_y[0], 1)
    else:
        terms_x = terms_x + pencil_along_y(diffusivity, fields)
        near = lax.ppermute(near, "row", [(i, i ^ 1) for i in range(rows) if i ^ 1 < rows])
    tendency, arrivals = total(gathered, row, column, terms_x, far, side_particles(terms_z), near, terms_z)
    return (tendency, stored(kept), arrivals.transpose(1, 0, 2))


def solution(mesh):
    return jax.shard_map(
        on_device,
        mesh=mesh,
        in_specs=(
            P(None, "row", None, "col"),
            P(),
            P(None, ("row", "col")),
            P(("row", "col")),
            P(("row", "col")),
            P(("row", "col")),
            P(("row", "col")),
            P(("row", "col")),
        ),
        out_specs=(
            P(None, "row", None, "col"),
            P(None, ("row", "col")),
            P(None, None, ("row", "col")),
        ),
        check_vma=False,
    )
```
